256 devices in a mesh: row: 4 (over x), col: 32 (over z, y), depth: 2 (over core).
Axes of the slice: x: 4, y: 4, z: 8, core: 2. Of those that a mesh axis runs over, the one named last changes fastest.
Arguments:
- tokens: bfloat16 [8192, 3200], P(('depth', 'col'), 'row'), may hold values from -6 to 6
- gain: bfloat16 [3200], P('row'), may hold values from 0.099609375 to 1.8984375
- w_up: bfloat16 [3200, 6400], P('col', 'row'), may hold values from -0.10606602 to 0.10606602
- w_down: bfloat16 [6400, 3200], P('row', 'col'), may hold values from -0.1125 to 0.1125
- cotangent: bfloat16 [8192, 3200], P(('depth', 'col'), 'row'), may hold values from -11 to 11
Outputs:
- out: bfloat16 [8192, 3200], P(('depth', 'col'), 'row')
- d_tokens: bfloat16 [8192, 3200], P(('depth', 'col'), 'row')
- grad_up: float32 [3200, 6400], P('col', 'row')
- grad_down: float32 [6400, 3200], P('row', 'col')
- grad_gain: float32 [3200], P('row')
The draws below stay inside these ranges and needn't reach their ends.
All inputs are finite; a program needn't handle non-finite values.
Results may differ from the reference program's by a relative error of at most 0.0055.
Values may be sent and summed in bfloat16 or wider, within the bound.
A program may use at most 128 MiB of HBM per device.

```python
import math
import jax
import jax.numpy as jnp
from jax import lax

D = 3200
FF = 6400
TOKENS = 8192


def token_parts(key):
    key = jax.random.fold_in(key, 101)
    subkeys = jax.random.split(key, 1)
    normal_part = jnp.clip(jax.random.normal(subkeys[0], (TOKENS, D), jnp.float32), -6.0, 6.0)
    return normal_part


def weight_parts(key):
    key = jax.random.fold_in(key, 202)
    subkeys = jax.random.split(key, 1)
    normal_part = jnp.clip(jax.random.normal(subkeys[0], (D, FF), jnp.float32), -6.0, 6.0)
    return normal_part


def draw_tokens(key, part):
    normal_part = token_parts(key)
    return normal_part.astype(jnp.bfloat16)


def draw_cotangent(key, part):
    normal_part = token_parts(key)
    key = jax.random.fold_in(key, 2)
    subkeys = jax.random.split(key, 3)
    token_sign = jnp.where(jax.random.bernoulli(subkeys[0], 0.5, (TOKENS, 1)), 1.0, -1.0)
    magnitude = jnp.exp(jax.random.uniform(subkeys[1], (TOKENS, 1), jnp.float32, math.log(0.5), 0.0))
    feature_ramp = 0.5 * jnp.power(3.0, jnp.arange(D, dtype=jnp.float32) / max(D - 1, 1))
    source = normal_part
    jitter = jnp.clip(jax.random.normal(subkeys[2], (TOKENS, D), jnp.float32), -6.0, 6.0)
    return (0.8 * token_sign * magnitude * feature_ramp[None, :] * source + 0.6 * jitter).astype(jnp.bfloat16)


def draw_w_up(key, part):
    normal_part = weight_parts(key)
    source = normal_part
    return (source * D ** (-0.5)).astype(jnp.bfloat16)


def draw_w_down(key, part):
    normal_part = weight_parts(key)
    key = jax.random.fold_in(key, 4)
    source = normal_part
    jitter = jnp.clip(jax.random.normal(key, (FF, D), jnp.float32), -6.0, 6.0)
    return ((0.7 * source.T + 0.714 * jitter) * FF ** (-0.5)).astype(jnp.bfloat16)


def setup_inputs(seed: int = 0) -> dict:
    streams_of = jax.random.split(jax.random.key(seed), 6)
    tokens = draw_tokens(jax.random.fold_in(streams_of[5], 71), 0)
    gain = jnp.clip(1.0 + 0.18 * jax.random.normal(streams_of[1], (D,), jnp.float32), 0.099609375, 1.8984375).astype(jnp.bfloat16)
    w_up = draw_w_up(jax.random.fold_in(streams_of[5], 71), 0)
    w_down = draw_w_down(jax.random.fold_in(streams_of[5], 71), 0)
    cotangent = draw_cotangent(jax.random.fold_in(streams_of[5], 71), 0)
    return {"tokens": tokens, "gain": gain, "w_up": w_up, "w_down": w_down, "cotangent": cotangent}


EPS = 1e-06

def gelu_value(pre):
    return 0.5 * pre * (1.0 + lax.erf(pre / math.sqrt(2.0)))

def gelu_slope(pre):
    return 0.5 * (1.0 + lax.erf(pre / math.sqrt(2.0))) + pre * jnp.exp(-0.5 * pre * pre) / math.sqrt(2.0 * math.pi)

def reference(tokens, gain, w_up, w_down, cotangent):
    xfull = tokens.astype(jnp.float32)
    gain_f = gain.astype(jnp.float32)
    inv = lax.rsqrt(lax.optimization_barrier(jnp.mean(xfull * xfull, axis=1, keepdims=True)) + EPS)
    unit = xfull * inv
    normed = (unit * gain_f).astype(jnp.bfloat16)
    pre = jnp.dot(normed, w_up, preferred_element_type=jnp.float32)
    hidden = gelu_value(pre).astype(jnp.bfloat16)
    branch = jnp.dot(hidden, w_down, preferred_element_type=jnp.float32)
    out = (xfull + branch).astype(jnp.bfloat16)
    d_hidden = lax.dot_general(cotangent, w_down, (((1,), (1,)), ((), ())), preferred_element_type=jnp.float32)
    d_pre = (d_hidden * gelu_slope(pre)).astype(jnp.bfloat16)
    d_normed = lax.dot_general(d_pre, w_up, (((1,), (1,)), ((), ())), preferred_element_type=jnp.float32)
    d_unit = d_normed * gain_f
    mean_dot = lax.optimization_barrier(jnp.mean(d_unit * unit, axis=1, keepdims=True))
    d_tokens = (cotangent.astype(jnp.float32) + inv * (d_unit - unit * mean_dot)).astype(jnp.bfloat16)
    scale = TOKENS ** (-0.5)
    grad_up = lax.dot_general(normed, d_pre, (((0,), (0,)), ((), ())), preferred_element_type=jnp.float32) * scale
    grad_down = lax.dot_general(hidden, cotangent, (((0,), (0,)), ((), ())), preferred_element_type=jnp.float32) * scale
    grad_gain = lax.optimization_barrier(jnp.sum(d_normed * unit, axis=0)) * scale
    return (out, d_tokens, grad_up, grad_down, grad_gain)
```

```python
import math

import jax
import jax.numpy as jnp
from jax import lax
from jax.experimental import pallas as pl
from jax.experimental.pallas import tpu as pltpu
from jax.sharding import PartitionSpec as P

EPS = 1e-06
MESH = pl.DeviceIdType.MESH
F32, BF16 = jnp.float32, jnp.bfloat16

NX, NY, NZ = 4, 4, 8
D, FF, TOK = 3200, 6400, 8192
DX = D // NX
TB = 128
T = NY * TB
DZ = D // NZ
DC = D // (NY * NZ)
FS = FF // (NX * NY)
FP = 512
RP = 112
EX = 16
DE = DX + EX
SUBS = ((0, 208), (208, 192))
HALF = ((0, 400), (400, 400))
HALFE = ((0, 400), (400, 416))
ORDER = (2, 1, -1, 0)
ZORDER = (4, 3, -3, 2, -2, 1, -1, 0)


def gelu_value(pre):
    return 0.5 * pre * (1.0 + lax.erf(pre / math.sqrt(2.0)))


def gelu_slope(pre):
    return 0.5 * (1.0 + lax.erf(pre / math.sqrt(2.0))) + pre * jnp.exp(
        -0.5 * pre * pre
    ) / math.sqrt(2.0 * math.pi)


def dot(left, right, left_dim, right_dim):
    return lax.dot_general(
        left, right, (((left_dim,), (right_dim,)), ((), ())), preferred_element_type=F32
    )


class Messages:
    def __init__(self, send, recv):
        self.send, self.recv, self.n, self.live = send, recv, 0, []

    def start(self, src, dst, device):
        i = self.n
        self.n += 1
        cp = pltpu.make_async_remote_copy(
            src_ref=src, dst_ref=dst, send_sem=self.send.at[i], recv_sem=self.recv.at[i],
            device_id=device, device_id_type=MESH,
        )
        cp.start()
        self.live.append(cp)
        return cp

    def drain(self):
        for cp in self.live:
            cp.wait_send()
        self.live = []


N_MESSAGES = 176


def kernel(
    x_in, c_in, w_in, g_in,
    out_ref, dtok_ref, gw_ref, gg_ref,
    xt, nc, w, wa, gr, gcol, inv_s, pre_s, dh_s, hd, md_s, g, xr, zs, zr,
    br, dn, b0, b1, bq0, bq1, d0, d1, dq0, dq1, stage, ga,
    send_sem, recv_sem, copy_sem,
):
    x = lax.axis_index("row")
    col = lax.axis_index("col")
    d = lax.axis_index("depth")
    y, z = lax.rem(col, NY), col // NY
    e = 1 - d

    def dev(ax=None, off=0):
        xx, yy, zz, dd = x, y, z, d
        if ax == "x":
            xx = lax.rem(x + (off + NX), NX)
        elif ax == "y":
            yy = lax.rem(y + (off + NY), NY)
        elif ax == "z":
            zz = lax.rem(z + (off + NZ), NZ)
        elif ax == "c":
            dd = e
        return (xx, zz * NY + yy, dd)

    def px(off):
        return lax.rem(x + (off + NX), NX)

    def py(off):
        return lax.rem(y + (off + NY), NY)

    def pz(off):
        return lax.rem(z + (off + NZ), NZ)

    def rows(i, size, off=0, n=None):
        return pl.ds(pl.multiple_of(i * size + off, 16), size if n is None else n)

    def lanes(i):
        return pl.ds(pl.multiple_of(i * TB, TB), TB)

    msg = Messages(send_sem, recv_sem)

    barrier = pltpu.get_barrier_semaphore()
    partners = [("x", 1), ("x", -1), ("x", 2), ("y", 1), ("y", -1), ("y", 2), ("z", 1), ("z", -1), ("c", 0)]
    for ax, off in partners:
        pl.semaphore_signal(barrier, inc=1, device_id=dev(ax, off), device_id_type=MESH)

    xt[rows(x, DX), lanes(y)] = x_in[...]
    nc[1, rows(x, DX), lanes(y)] = c_in[...]
    gr[x] = g_in[...]
    pl.semaphore_wait(barrier, len(partners))

    class Gather:
        def __init__(self, ref, first, second):
            self.ref, self.a, self.b = ref, first, second
            self.n1, self.n2 = {}, {}

        def at(self, a, b, half=None):
            xi, yi = (px(a), py(b)) if self.a == "x" else (px(b), py(a))
            off, n = (0, DX) if half is None else HALF[half]
            return self.ref(rows(xi, DX, off, n), lanes(yi))

        def go(self, a, b, ax, off, half=None):
            ref = self.at(a, b, half)
            return msg.start(ref, ref, dev(ax, off))

        def first(self):
            self.m1 = [self.go(0, 0, self.a, 1), self.go(0, 0, self.a, -1)]

        def second(self, a):
            self.n1[a] = [self.go(a, 0, self.b, 1), self.go(a, 0, self.b, -1)]

        def first_forward(self):
            self.m1[0].wait_recv()
            m2p = self.go(-1, 0, self.a, 1, 0)
            self.m1[1].wait_recv()
            m2m = self.go(1, 0, self.a, -1, 1)
            self.m2 = [m2p, m2m]

        def first_done(self):
            for cp in self.m2:
                cp.wait_recv()

        def second_forward(self, a):
            self.n1[a][0].wait_recv()
            p = self.go(a, -1, self.b, 1, 0)
            self.n1[a][1].wait_recv()
            m = self.go(a, 1, self.b, -1, 1)
            self.n2[a] = [p, m]

        def second_done(self, a):
            for cp in self.n2[a]:
                cp.wait_recv()

    gx = Gather(lambda r, l: xt.at[r, l], "x", "y")
    gc = Gather(lambda r, l: nc.at[1, r, l], "y", "x")

    gain_msgs = [msg.start(g_in, gr.at[x], dev("x", off)) for off in (1, -1, 2)]
    a2a = [msg.start(w_in.at[d, py(off)], wa.at[y], dev("y", off)) for off in (1, -1, 2)]
    gx.first()
    gc.first()
    gx.second(0)
    gc.second(0)
    wa[y] = w_in[d, y]

    r_i = lax.broadcasted_iota(jnp.int32, (DZ, NY * RP), 0)
    c_i = lax.broadcasted_iota(jnp.int32, (DZ, NY * RP), 1)
    shift = jnp.where(r_i >= 3 * DC, 3, jnp.where(r_i >= 2 * DC, 2, jnp.where(r_i >= DC, 1, 0)))
    select = jnp.where(c_i == r_i + (RP - DC) * shift, 1.0, 0.0).astype(BF16)

    for cp in a2a:
        cp.wait_recv()
    w[d, rows(z, DZ)] = dot(select, wa[...].reshape(NY * RP, FP), 1, 0).astype(BF16)

    def w_at(off, sub):
        o, n = SUBS[sub]
        return w.at[d, rows(pz(off), DZ, o, n)]

    zp, zm, wc = {}, {}, []

    def z_send(s):
        for sub in (0, 1):
            if s < 3 or sub == 0:
                zp[s, sub] = msg.start(w_at(-s, sub), w_at(-s, sub), dev("z", 1))
            if s < 3 or sub == 1:
                zm[s, sub] = msg.start(w_at(s, sub), w_at(s, sub), dev("z", -1))

    def z_step(s):
        for sub in (0, 1):
            if (s, sub) in zp:
                zp[s, sub].wait_recv()
                if s < 2 or (s == 2 and sub == 0):
                    ref = w_at(-(s + 1), sub)
                    zp[s + 1, sub] = msg.start(ref, ref, dev("z", 1))
            if (s, sub) in zm:
                zm[s, sub].wait_recv()
                if s < 2 or (s == 2 and sub == 1):
                    ref = w_at(s + 1, sub)
                    zm[s + 1, sub] = msg.start(ref, ref, dev("z", -1))
            if (s, sub) in zp:
                ref = w_at(-(s + 1), sub)
                wc.append(msg.start(ref, ref, dev("c")))
            if (s, sub) in zm:
                ref = w_at(s + 1, sub)
                wc.append(msg.start(ref, ref, dev("c")))

    z_send(0)
    for sub in (0, 1):
        ref = w_at(0, sub)
        wc.append(msg.start(ref, ref, dev("c")))

    gx.first_forward()
    gc.first_forward()
    for a in (-1, 1):
        gx.second(a)
        gc.second(a)
    for cp in gain_msgs:
        cp.wait_recv()

    def spread_gain(i, carry):
        column = gr[i].T[:DX, 0:1]
        gcol[i] = jnp.broadcast_to(column, (DX, TB))
        return carry

    lax.fori_loop(0, NX, spread_gain, 0)

    def normalise(off):
        yi = py(off)

        def square(i, acc):
            v = xt[pl.ds(pl.multiple_of(i * 160, 16), 160), lanes(yi)].astype(F32)
            return acc + jnp.sum(v * v, axis=0, keepdims=True)

        total = lax.fori_loop(0, D // 160, square, jnp.zeros((1, TB), F32))
        inv = lax.rsqrt(total / D + EPS)
        if off == 0:
            inv_s[...] = inv

        def scale(i, carry):
            xi, k = i // 5, lax.rem(i, 5)
            r = pl.ds(pl.multiple_of(i * 160, 16), 160)
            v = xt[r, lanes(yi)].astype(F32) * inv
            nc[0, r, lanes(yi)] = (v * gcol[xi, pl.ds(pl.multiple_of(k * 160, 16), 160)]).astype(BF16)
            return carry

        lax.fori_loop(0, D // 160, scale, 0)

    gx.first_done()
    gx.second(2)
    gc.first_done()
    gc.second(2)
    normalise(0)
    gx.second_forward(0)
    gc.second_forward(0)
    z_step(0)
    for a in (-1, 1):
        gx.second_forward(a)
        gc.second_forward(a)
    z_step(1)
    gx.second_forward(2)
    gc.second_forward(2)
    normalise(1)
    normalise(-1)
    z_step(2)
    for a in (0, -1, 1, 2):
        gx.second_done(a)
    normalise(2)
    for a in (0, -1, 1, 2):
        gc.second_done(a)
    z_step(3)
    for cp in wc:
        cp.wait_recv()
    msg.drain()

    pre_s[...] = jnp.zeros_like(pre_s)
    dh_s[...] = jnp.zeros_like(dh_s)

    def up(i, carry):
        r = rows(i, DZ)
        pre_s[...] += dot(w[0, r], nc[0, r], 0, 0)
        dh_s[...] += dot(w[1, r], nc[1, r], 0, 0)
        return carry

    lax.fori_loop(0, NZ, up, 0)

    hd[0, pl.ds(FS, FP - FS)] = jnp.zeros((FP - FS, T), BF16)
    hd[1, pl.ds(FS, FP - FS)] = jnp.zeros((FP - FS, T), BF16)

    def act(i, acc):
        r = pl.ds(pl.multiple_of(i * 16, 16), 16)
        pre = pre_s[r]
        dpre = dh_s[r] * gelu_slope(pre)
        hd[1, r] = gelu_value(pre).astype(BF16)
        hd[0, r] = dpre.astype(BF16)
        return acc + jnp.sum(dpre * pre, axis=0, keepdims=True)

    md_s[...] = lax.fori_loop(0, FS // 16, act, jnp.zeros((1, T), F32))

    core = {}

    def grad_chunk(k):
        r = rows(pz(ZORDER[k]), DZ)
        xt[pl.ds(k * DZ, DZ)] = dot(nc[e, r], hd[e], 1, 1).astype(BF16)
        core[k] = msg.start(xt.at[pl.ds(k * DZ, DZ)], xr.at[k], dev("c"))
        g[k] = dot(nc[d, r], hd[d], 1, 1)

    zmsg = {}

    def z_reduce(s, k, p):
        for sub in (0, 1):
            if s == 0 and sub != p:
                continue
            o, n = SUBS[sub]
            r = pl.ds(o, n)
            val = g[k, r] + xr[k, r].astype(F32)
            if (p, s - 1, sub) in zmsg:
                zmsg[p, s - 1, sub].wait_recv()
                val = val + zr[p, s - 1, r].astype(F32)
            zs[p, s, r] = val.astype(BF16)
            zmsg[p, s, sub] = msg.start(zs.at[p, s, r], zr.at[p, s, r], dev("z", 1 - 2 * p))

    class Reduce:
        def __init__(self, ref, a, b, halves, r0, r1, q0, q1):
            self.ref, self.a, self.b, self.h = ref, a, b, halves
            self.r0, self.r1, self.q0, self.q1 = r0, r1, q0, q1
            self.p0, self.p1 = {}, {}

        def at(self, a, b):
            return (px(a), py(b)) if self.a == "x" else (px(b), py(a))

        def send0(self, b):
            i = ORDER.index(b)
            xi, yi = self.at(2, b)
            self.p0[b] = []
            for s in (0, 1):
                o, n = self.h[s]
                self.p0[b].append(msg.start(
                    self.ref.at[xi, yi, pl.ds(o, n)], self.r0.at[i, s, pl.ds(0, n)], dev(self.a, 1 - 2 * s)))

        def send1(self, b):
            i = ORDER.index(b)
            self.p1[b] = []
            for s in (0, 1):
                o, n = self.h[s]
                xi, yi = self.at(1 - 2 * s, b)
                self.p0[b][s].wait_recv()
                self.ref[xi, yi, pl.ds(o, n)] = (
                    self.ref[xi, yi, pl.ds(o, n)].astype(F32) + self.r0[i, s, pl.ds(0, n)].astype(F32)
                ).astype(BF16)
                self.p1[b].append(msg.start(self.ref.at[xi, yi], self.r1.at[i, s], dev(self.a, 1 - 2 * s)))

        def sum1(self, b):
            i = ORDER.index(b)
            xi, yi = self.at(0, b)
            for s in (0, 1):
                self.p1[b][s].wait_recv()
            return self.ref[xi, yi].astype(F32) + self.r1[i, 0].astype(F32) + self.r1[i, 1].astype(F32)

        def second0(self):
            xi, yi = self.at(0, 2)
            self.ref[xi, yi] = self.sum1(2).astype(BF16)
            self.m0 = []
            for s in (0, 1):
                o, n = self.h[s]
                self.m0.append(msg.start(
                    self.ref.at[xi, yi, pl.ds(o, n)], self.q0.at[s, pl.ds(0, n)], dev(self.b, 1 - 2 * s)))

        def second1(self):
            self.m1 = []
            for s in (0, 1):
                b = 1 - 2 * s
                xi, yi = self.at(0, b)
                o, n = self.h[s]
                total = self.sum1(b)
                self.m0[s].wait_recv()
                other = slice(n, None) if o == 0 else slice(0, o)
                self.ref[xi, yi, pl.ds(o, n)] = (
                    total[o:o + n] + self.q0[s, pl.ds(0, n)].astype(F32)).astype(BF16)
                so, sn = self.h[1 - s]
                self.ref[xi, yi, pl.ds(so, sn)] = total[other].astype(BF16)
                self.m1.append(msg.start(self.ref.at[xi, yi], self.q1.at[s], dev(self.b, b)))

        def result(self):
            total = self.sum1(0)
            for s in (0, 1):
                self.m1[s].wait_recv()
            return total + self.q1[0].astype(F32) + self.q1[1].astype(F32)

    rb = Reduce(br, "y", "x", HALF, b0, b1, bq0, bq1)
    rd = Reduce(dn, "x", "y", HALFE, d0, d1, dq0, dq1)

    def branch_block(off):
        xi = px(off)
        val = dot(w[1, rows(xi, DX)], hd[1], 1, 0).astype(BF16)
        for j in range(NY):
            br[xi, j] = val[:, j * TB:(j + 1) * TB]

    def normed_block(off):
        xi = px(off)
        val = dot(w[0, rows(xi, DX)], hd[0], 1, 0).astype(BF16)
        for j in range(NY):
            dn[xi, j, pl.ds(0, DX)] = val[:, j * TB:(j + 1) * TB]
            dn[xi, j, pl.ds(DX, EX)] = jnp.broadcast_to(
                md_s[:, j * TB:(j + 1) * TB], (EX, TB)).astype(BF16)

    grad_chunk(0)
    branch_block(2)
    rb.send0(2)
    normed_block(2)
    for b in ORDER:
        rd.send0(b)
    core[0].wait_recv()
    z_reduce(0, 0, 0)
    z_reduce(0, 0, 1)
    branch_block(1)
    rb.send0(1)
    branch_block(-1)
    rb.send0(-1)
    branch_block(0)
    rb.send0(0)
    grad_chunk(1)
    grad_chunk(2)
    normed_block(1)
    normed_block(-1)
    rb.send1(2)
    rd.send1(2)
    for k in (1, 2):
        core[k].wait_recv()
    z_reduce(1, 1, 0)
    z_reduce(1, 2, 1)
    normed_block(0)
    for b in (1, -1, 0):
        rb.send1(b)
        rd.send1(b)
    for k in (3, 4):
        grad_chunk(k)
    rb.second0()
    rd.second0()
    for k in (3, 4):
        core[k].wait_recv()
    z_reduce(2, 3, 0)
    z_reduce(2, 4, 1)
    for k in (5, 6, 7):
        grad_chunk(k)
    rb.second1()
    rd.second1()
    for k in (5, 6):
        core[k].wait_recv()
    z_reduce(3, 5, 0)
    z_reduce(3, 6, 1)

    xf = x_in[...].astype(F32)
    out_ref[...] = (xf + rb.result()).astype(BF16)
    total = rd.result()
    dnorm = total[:DX]
    inv = inv_s[...]
    mean_dot = total[DX:DX + 1] / D
    unit = xf * inv
    dtok_ref[...] = (
        c_in[...].astype(F32) + inv * (dnorm * gcol[x] - unit * mean_dot)
    ).astype(BF16)
    gg_ref[...] = jnp.sum(dnorm * unit, axis=1, keepdims=True)

    core[7].wait_recv()
    for p in (0, 1):
        for sub in (0, 1):
            zmsg[p, 3, sub].wait_recv()
    final = (
        g[7] + xr[7].astype(F32) + zr[0, 3].astype(F32) + zr[1, 3].astype(F32)
    ).astype(BF16)
    stage[...] = dot(select, final, 0, 0).astype(BF16).reshape(NY, RP, FP)
    back = [msg.start(stage.at[py(off)], ga.at[d, y], dev("y", off)) for off in (1, -1, 2)]
    ga[d, y] = stage[y]
    hand = [msg.start(ga.at[d, y], ga.at[d, y], dev("c"))]
    for cp, off in zip(back, (1, -1, 2)):
        cp.wait_recv()
        ref = ga.at[d, py(-off)]
        hand.append(msg.start(ref, ref, dev("c")))
    for cp in hand:
        cp.wait_recv()
    gw_ref[...] = ga[...]
    msg.drain()


def vm(shape, dtype=BF16):
    return pltpu.VMEM(shape, dtype)


def block(xt, ct, w, g):
    spec = pl.BlockSpec(memory_space=pltpu.VMEM)
    return pl.pallas_call(
        kernel,
        out_shape=(
            jax.ShapeDtypeStruct((DX, TB), BF16),
            jax.ShapeDtypeStruct((DX, TB), BF16),
            jax.ShapeDtypeStruct((2, NY, RP, FP), BF16),
            jax.ShapeDtypeStruct((DX, 1), F32),
        ),
        in_specs=[spec] * 4,
        out_specs=(spec,) * 4,
        scratch_shapes=[
            vm((D, T)),
            vm((2, D, T)),
            vm((2, D, FP)),
            vm((NY, RP, FP)),
            vm((NX, 8, 896), F32),
            vm((NX, DX, TB), F32),
            vm((1, TB), F32),
            vm((FP, T), F32),
            vm((FP, T), F32),
            vm((2, FP, T)),
            vm((1, T), F32),
            vm((NZ, DZ, FP), F32),
            vm((NZ, DZ, FP)),
            vm((2, 4, DZ, FP)),
            vm((2, 4, DZ, FP)),
            vm((NX, NY, DX, TB)),
            vm((NX, NY, DE, TB)),
            vm((4, 2, 400, TB)),
            vm((4, 2, DX, TB)),
            vm((2, 400, TB)),
            vm((2, DX, TB)),
            vm((4, 2, 416, TB)),
            vm((4, 2, DE, TB)),
            vm((2, 416, TB)),
            vm((2, DE, TB)),
            vm((NY, RP, FP)),
            vm((2, NY, RP, FP)),
            pltpu.SemaphoreType.DMA((N_MESSAGES,)),
            pltpu.SemaphoreType.DMA((N_MESSAGES,)),
            pltpu.SemaphoreType.DMA,
        ],
        compiler_params=pltpu.CompilerParams(
            collective_id=0, has_side_effects=True, vmem_limit_bytes=60 * 2**20
        ),
    )(xt, ct, w, g)


def on_device(tokens, gain, w_up, w_down, cotangent):
    up = w_up.reshape(DC, NY, FS).transpose(1, 0, 2)
    down = w_down.reshape(NY, FS, DC).transpose(0, 2, 1)
    w = jnp.pad(jnp.stack([up, down]), ((0, 0), (0, 0), (0, RP - DC), (0, FP - FS)))
    g = jnp.broadcast_to(jnp.pad(gain.astype(F32), (0, 896 - DX))[None], (8, 896))
    out_t, dtok_t, gw, gg = block(tokens.T, cotangent.T, w, g)
    scale = TOK ** (-0.5)
    gw = gw[:, :, :DC, :FS].astype(F32) * scale
    grad_up = gw[0].transpose(1, 0, 2).reshape(DC, NY * FS)
    grad_down = gw[1].transpose(0, 2, 1).reshape(NY * FS, DC)
    grad_gain = lax.psum(gg[:, 0], ("col", "depth")) * scale
    return out_t.T, dtok_t.T, grad_up, grad_down, grad_gain


def solution(mesh):
    in_specs = (
        P(("depth", "col"), "row"),
        P("row"),
        P("col", "row"),
        P("row", "col"),
        P(("depth", "col"), "row"),
    )
    out_specs = (
        P(("depth", "col"), "row"),
        P(("depth", "col"), "row"),
        P("col", "row"),
        P("row", "col"),
        P("row"),
    )
    return jax.shard_map(
        on_device, mesh=mesh, in_specs=in_specs, out_specs=out_specs, check_vma=False
    )
```

```python
import math

import jax
import jax.numpy as jnp
from jax import lax
from jax.experimental import pallas as pl
from jax.experimental.pallas import tpu as pltpu
from jax.sharding import PartitionSpec as P

EPS = 1e-06
MESH = pl.DeviceIdType.MESH
F32, BF16 = jnp.float32, jnp.bfloat16

NX, NY, NZ = 4, 4, 8
D, FF, TOK = 3200, 6400, 8192
DX = D // NX
TB = 128
T = NY * TB
DZ = D // NZ
DC = D // (NY * NZ)
FS = FF // (NX * NY)
FP = 512
RP = 112
EX = 16
DE = DX + EX
FM = 384
ZP = 432
SUBS = ((0, 208), (208, 224))
HALF = ((0, 400), (400, 400))
HALFE = ((0, 400), (400, 416))
ORDER = (2, 1, -1, 0)
ZORDER = (4, 3, -3, 2, -2, 1, -1, 0)
SCALE = TOK ** (-0.5)


def gelu_value(pre):
    return 0.5 * pre * (1.0 + lax.erf(pre / math.sqrt(2.0)))


def gelu_slope(pre):
    return 0.5 * (1.0 + lax.erf(pre / math.sqrt(2.0))) + pre * jnp.exp(
        -0.5 * pre * pre
    ) / math.sqrt(2.0 * math.pi)


def dot(left, right, left_dim, right_dim):
    return lax.dot_general(
        left, right, (((left_dim,), (right_dim,)), ((), ())), preferred_element_type=F32
    )


class Messages:
    def __init__(self, send, recv):
        self.send, self.recv, self.n, self.live = send, recv, 0, []

    def start(self, src, dst, device):
        i = self.n
        self.n += 1
        cp = pltpu.make_async_remote_copy(
            src_ref=src, dst_ref=dst, send_sem=self.send.at[i], recv_sem=self.recv.at[i],
            device_id=device, device_id_type=MESH,
        )
        cp.start()
        self.live.append(cp)
        return cp

    def drain(self):
        for cp in self.live:
            cp.wait_send()
        self.live = []


N_MESSAGES = 176


def kernel(
    x_in, c_in, up_in, down_in, g_in,
    out_hbm, dtok_hbm, gu_hbm, gd_hbm, gg_ref,
    xo, co, ws, w_in, wz, out_ref, dtok_ref, gu_ref, gd_ref, xt, nc, w, wa, gr, gcol, inv_s, pre_s, dh_s, hd, md_s, gs, g, xr, zs, zr,
    br, dn, b0, b1, bq0, bq1, d0, d1, dq0, dq1, stage, ga, ggp, ggr, ggx, ggy, ggz, ggc,
    send_sem, recv_sem, copy_sem,
):
    x = lax.axis_index("row")
    col = lax.axis_index("col")
    d = lax.axis_index("depth")
    y, z = lax.rem(col, NY), col // NY
    e = 1 - d

    def dev(ax=None, off=0):
        xx, yy, zz, dd = x, y, z, d
        if ax == "x":
            xx = lax.rem(x + (off + NX), NX)
        elif ax == "y":
            yy = lax.rem(y + (off + NY), NY)
        elif ax == "z":
            zz = lax.rem(z + (off + NZ), NZ)
        elif ax == "c":
            dd = e
        return (xx, zz * NY + yy, dd)

    def px(off):
        return lax.rem(x + (off + NX), NX)

    def py(off):
        return lax.rem(y + (off + NY), NY)

    def pz(off):
        return lax.rem(z + (off + NZ), NZ)

    def rows(i, size, off=0, n=None):
        return pl.ds(pl.multiple_of(i * size + off, 16), size if n is None else n)

    def lanes(i):
        return pl.ds(pl.multiple_of(i * TB, TB), TB)

    msg = Messages(send_sem, recv_sem)

    barrier = pltpu.get_barrier_semaphore()
    partners = [("x", 1), ("x", -1), ("x", 2), ("y", 1), ("y", -1), ("y", 2), ("z", 1), ("z", -1), ("c", 0)]
    for ax, off in partners:
        pl.semaphore_signal(barrier, inc=1, device_id=dev(ax, off), device_id_type=MESH)

    loads = [pltpu.make_async_copy(x_in, xo, copy_sem.at[0]), pltpu.make_async_copy(c_in, co, copy_sem.at[1])]
    for cp in loads:
        cp.start()

    @pl.when(d == 0)
    def _():
        cp = pltpu.make_async_copy(up_in, ws, copy_sem.at[2])
        cp.start()
        cp.wait()

    @pl.when(d == 1)
    def _():
        cp = pltpu.make_async_copy(down_in, ws, copy_sem.at[2])
        cp.start()
        cp.wait()

    w_in[...] = jnp.zeros_like(w_in)
    for j in range(NY):
        w_in[j, pl.ds(0, DC), pl.ds(0, FS)] = ws[:, j * FS:(j + 1) * FS]
    for cp in loads:
        cp.wait()
    xt[rows(x, DX), lanes(y)] = xo[...]
    nc[1, rows(x, DX), lanes(y)] = co[...]
    gain_own = g_in[...].astype(F32)
    gr[x] = jnp.zeros_like(gr[0])
    gr[x, :, pl.ds(0, DX)] = jnp.broadcast_to(gain_own, (8, DX))
    pl.semaphore_wait(barrier, len(partners))

    class Gather:
        def __init__(self, ref, first, second):
            self.ref, self.a, self.b = ref, first, second
            self.n1, self.n2 = {}, {}

        def at(self, a, b, half=None):
            xi, yi = (px(a), py(b)) if self.a == "x" else (px(b), py(a))
            off, n = (0, DX) if half is None else HALF[half]
            return self.ref(rows(xi, DX, off, n), lanes(yi))

        def go(self, a, b, ax, off, half=None):
            ref = self.at(a, b, half)
            return msg.start(ref, ref, dev(ax, off))

        def first(self):
            self.m1 = [self.go(0, 0, self.a, 1), self.go(0, 0, self.a, -1)]

        def second(self, a):
            self.n1[a] = [self.go(a, 0, self.b, 1), self.go(a, 0, self.b, -1)]

        def first_forward(self):
            self.m1[0].wait_recv()
            m2p = self.go(-1, 0, self.a, 1, 0)
            self.m1[1].wait_recv()
            m2m = self.go(1, 0, self.a, -1, 1)
            self.m2 = [m2p, m2m]

        def first_done(self):
            for cp in self.m2:
                cp.wait_recv()

        def second_forward(self, a):
            self.n1[a][0].wait_recv()
            p = self.go(a, -1, self.b, 1, 0)
            self.n1[a][1].wait_recv()
            m = self.go(a, 1, self.b, -1, 1)
            self.n2[a] = [p, m]

        def second_done(self, a):
            for cp in self.n2[a]:
                cp.wait_recv()

    gx = Gather(lambda r, l: xt.at[r, l], "x", "y")
    gc = Gather(lambda r, l: nc.at[1, r, l], "y", "x")

    gain_msgs = [msg.start(gr.at[x], gr.at[x], dev("x", off)) for off in (1, -1, 2)]
    a2a = [msg.start(w_in.at[py(off)], wa.at[y], dev("y", off)) for off in (1, -1, 2)]
    gx.first()
    gc.first()
    gx.second(0)
    gc.second(0)
    wa[y] = w_in[y]

    r_i = lax.broadcasted_iota(jnp.int32, (DZ, NY * RP), 0)
    c_i = lax.broadcasted_iota(jnp.int32, (DZ, NY * RP), 1)
    shift = jnp.where(r_i >= 3 * DC, 3, jnp.where(r_i >= 2 * DC, 2, jnp.where(r_i >= DC, 1, 0)))
    select = jnp.where(c_i == r_i + (RP - DC) * shift, 1.0, 0.0).astype(BF16)

    for cp in a2a:
        cp.wait_recv()
    own = dot(select, wa[...].reshape(NY * RP, FP), 1, 0)
    w[d, rows(z, DZ)] = own.astype(BF16)

    def pack(ref, i, val):
        tail = jnp.concatenate([val[:, FM:], jnp.zeros((FP - DZ, FP - FM), F32)], axis=0).T[:16]
        ref[i, pl.ds(0, DZ)] = val[:, :FM].astype(ref.dtype)
        ref[i, pl.ds(DZ, 16)] = tail[:, :FM].astype(ref.dtype)
        ref[i, pl.ds(DZ + 16, 16), pl.ds(0, FP - FM)] = tail[:, FM:].astype(ref.dtype)

    def tail_of(val):
        tail = jnp.concatenate([val[DZ:DZ + 16], val[DZ + 16:, :FP - FM]], axis=1)
        tail = jnp.concatenate([tail, jnp.zeros((FP - FM - 16, FP), F32)], axis=0)
        return tail.T[:DZ]

    wz[z, pl.ds(DZ + 16, 16), :] = jnp.zeros((16, FM), BF16)
    pack(wz, z, own)

    def w_at(off, sub):
        o, n = SUBS[sub]
        return wz.at[pz(off), pl.ds(o, n)]

    def hand(off):
        ref = w.at[d, rows(pz(off), DZ)]
        wc.append(msg.start(ref, ref, dev("c")))

    def unpack(off):
        r = rows(pz(off), DZ)
        w[d, r, pl.ds(0, FM)] = wz[pz(off), pl.ds(0, DZ)]
        w[d, r, pl.ds(FM, FP - FM)] = tail_of(wz[pz(off)].astype(F32)).astype(BF16)
        hand(off)

    zp, zm, wc = {}, {}, []

    def z_send(s):
        for sub in (0, 1):
            if s < 3 or sub == 0:
                zp[s, sub] = msg.start(w_at(-s, sub), w_at(-s, sub), dev("z", 1))
            if s < 3 or sub == 1:
                zm[s, sub] = msg.start(w_at(s, sub), w_at(s, sub), dev("z", -1))

    def z_step(s):
        for sub in (0, 1):
            if (s, sub) in zp:
                zp[s, sub].wait_recv()
                if s < 2 or (s == 2 and sub == 0):
                    ref = w_at(-(s + 1), sub)
                    zp[s + 1, sub] = msg.start(ref, ref, dev("z", 1))
            if (s, sub) in zm:
                zm[s, sub].wait_recv()
                if s < 2 or (s == 2 and sub == 1):
                    ref = w_at(s + 1, sub)
                    zm[s + 1, sub] = msg.start(ref, ref, dev("z", -1))
        unpack(s + 1)
        if s < 3:
            unpack(-(s + 1))

    z_send(0)
    hand(0)

    gx.first_forward()
    gc.first_forward()
    for a in (-1, 1):
        gx.second(a)
        gc.second(a)
    for cp in gain_msgs:
        cp.wait_recv()

    def spread_gain(i, carry):
        column = gr[i].T[:DX, 0:1]
        gcol[i] = jnp.broadcast_to(column, (DX, TB))
        return carry

    lax.fori_loop(0, NX, spread_gain, 0)

    def normalise(off):
        yi = py(off)

        def square(i, acc):
            v = xt[pl.ds(pl.multiple_of(i * 160, 16), 160), lanes(yi)].astype(F32)
            return acc + jnp.sum(v * v, axis=0, keepdims=True)

        total = lax.fori_loop(0, D // 160, square, jnp.zeros((1, TB), F32))
        inv = lax.rsqrt(total / D + EPS)
        if off == 0:
            inv_s[...] = inv

        def scale(i, carry):
            xi, k = i // 5, lax.rem(i, 5)
            r = pl.ds(pl.multiple_of(i * 160, 16), 160)
            v = xt[r, lanes(yi)].astype(F32) * inv
            nc[0, r, lanes(yi)] = (v * gcol[xi, pl.ds(pl.multiple_of(k * 160, 16), 160)]).astype(BF16)
            return carry

        lax.fori_loop(0, D // 160, scale, 0)

    gx.first_done()
    gx.second(2)
    gc.first_done()
    gc.second(2)
    normalise(0)
    gx.second_forward(0)
    gc.second_forward(0)
    z_step(0)
    for a in (-1, 1):
        gx.second_forward(a)
        gc.second_forward(a)
    z_step(1)
    gx.second_forward(2)
    gc.second_forward(2)
    normalise(1)
    normalise(-1)
    z_step(2)
    for a in (0, -1, 1, 2):
        gx.second_done(a)
    normalise(2)
    for a in (0, -1, 1, 2):
        gc.second_done(a)
    z_step(3)
    for cp in wc:
        cp.wait_recv()
    msg.drain()

    pre_s[...] = jnp.zeros_like(pre_s)
    dh_s[...] = jnp.zeros_like(dh_s)

    def up(i, carry):
        r = rows(i, DZ)
        pre_s[...] += dot(w[0, r], nc[0, r], 0, 0)
        dh_s[...] += dot(w[1, r], nc[1, r], 0, 0)
        return carry

    lax.fori_loop(0, NZ, up, 0)

    hd[0, pl.ds(FS, FP - FS)] = jnp.zeros((FP - FS, T), BF16)
    hd[1, pl.ds(FS, FP - FS)] = jnp.zeros((FP - FS, T), BF16)

    def act(i, acc):
        r = pl.ds(pl.multiple_of(i * 16, 16), 16)
        pre = pre_s[r]
        dpre = dh_s[r] * gelu_slope(pre)
        hd[1, r] = gelu_value(pre).astype(BF16)
        hd[0, r] = dpre.astype(BF16)
        return acc + jnp.sum(dpre * pre, axis=0, keepdims=True)

    md_s[...] = lax.fori_loop(0, FS // 16, act, jnp.zeros((1, T), F32))

    core = {}
    ggr[...] = jnp.zeros_like(ggr)
    g[:, pl.ds(DZ + 16, 16), :] = jnp.zeros((NZ, 16, FM), F32)
    ones = jnp.ones((8, FP), BF16)

    def fold(k):
        core[k].wait_recv()
        zc = pz(ZORDER[k])
        total = gs[k] + xr[k].astype(F32)
        pack(g, k, total)
        v = total * w[d, rows(zc, DZ)].astype(F32)
        high = v.astype(BF16)
        low = (v - high.astype(F32)).astype(BF16)
        ggr[:, pl.ds(0, DZ)] = dot(ones, high, 1, 1) + dot(ones, low, 1, 1)
        for j in range(4):
            ggp[zc // 2, pl.ds(lax.rem(zc, 2) * 4 + j, 1), :] = ggr[0:1, j * TB:(j + 1) * TB]

    def gain_x():
        return [msg.start(ggp.at[px(off)], ggx.at[i], dev("x", off)) for i, off in enumerate((1, -1, 2))]

    def gain_y(cps):
        for cp in cps:
            cp.wait_recv()
        ggy[0] = ggp[x] + ggx[0] + ggx[1] + ggx[2]
        return [msg.start(ggy.at[0], ggy.at[1 + i], dev("y", off)) for i, off in enumerate((1, -1, 2))]

    def gain_z(cps):
        for cp in cps:
            cp.wait_recv()
        ggz[0] = ggy[0] + ggy[1] + ggy[2] + ggy[3]
        return [msg.start(ggz.at[0], ggz.at[1 + p], dev("z", 1 - 2 * p)) for p in (0, 1)]

    def gain_ring(cps, s):
        for cp in cps:
            cp.wait_recv()
        return [
            msg.start(ggz.at[2 * s - 1 + p], ggz.at[2 * s + 1 + p], dev("z", 1 - 2 * p))
            for p in ((0, 1) if s < 3 else (0,))
        ]

    def gain_c(cps):
        for cp in cps:
            cp.wait_recv()
        total = ggz[0]
        for i in range(NZ - 1):
            total = total + ggz[1 + i]
        ggc[0] = total
        return [msg.start(ggc.at[0], ggc.at[1], dev("c"))]

    def grad_chunk(k):
        r = rows(pz(ZORDER[k]), DZ)
        xt[pl.ds(k * DZ, DZ)] = dot(nc[e, r], hd[e], 1, 1).astype(BF16)
        core[k] = msg.start(xt.at[pl.ds(k * DZ, DZ)], xr.at[k], dev("c"))
        gs[k] = dot(nc[d, r], hd[d], 1, 1)

    zmsg = {}

    def z_reduce(s, k, p):
        for sub in (0, 1):
            if s == 0 and sub != p:
                continue
            o, n = SUBS[sub]
            r = pl.ds(o, n)
            val = g[k, r]
            if (p, s - 1, sub) in zmsg:
                zmsg[p, s - 1, sub].wait_recv()
                val = val + zr[p, s - 1, r].astype(F32)
            zs[p, s, r] = val.astype(BF16)
            zmsg[p, s, sub] = msg.start(zs.at[p, s, r], zr.at[p, s, r], dev("z", 1 - 2 * p))

    class Reduce:
        def __init__(self, ref, a, b, halves, r0, r1, q0, q1):
            self.ref, self.a, self.b, self.h = ref, a, b, halves
            self.r0, self.r1, self.q0, self.q1 = r0, r1, q0, q1
            self.p0, self.p1 = {}, {}

        def at(self, a, b):
            return (px(a), py(b)) if self.a == "x" else (px(b), py(a))

        def send0(self, b):
            i = ORDER.index(b)
            xi, yi = self.at(2, b)
            self.p0[b] = []
            for s in (0, 1):
                o, n = self.h[s]
                self.p0[b].append(msg.start(
                    self.ref.at[xi, yi, pl.ds(o, n)], self.r0.at[i, s, pl.ds(0, n)], dev(self.a, 1 - 2 * s)))

        def send1(self, b):
            i = ORDER.index(b)
            self.p1[b] = []
            for s in (0, 1):
                o, n = self.h[s]
                xi, yi = self.at(1 - 2 * s, b)
                self.p0[b][s].wait_recv()
                self.ref[xi, yi, pl.ds(o, n)] = (
                    self.ref[xi, yi, pl.ds(o, n)].astype(F32) + self.r0[i, s, pl.ds(0, n)].astype(F32)
                ).astype(BF16)
                self.p1[b].append(msg.start(self.ref.at[xi, yi], self.r1.at[i, s], dev(self.a, 1 - 2 * s)))

        def sum1(self, b):
            i = ORDER.index(b)
            xi, yi = self.at(0, b)
            for s in (0, 1):
                self.p1[b][s].wait_recv()
            return self.ref[xi, yi].astype(F32) + self.r1[i, 0].astype(F32) + self.r1[i, 1].astype(F32)

        def second0(self):
            xi, yi = self.at(0, 2)
            self.ref[xi, yi] = self.sum1(2).astype(BF16)
            self.m0 = []
            for s in (0, 1):
                o, n = self.h[s]
                self.m0.append(msg.start(
                    self.ref.at[xi, yi, pl.ds(o, n)], self.q0.at[s, pl.ds(0, n)], dev(self.b, 1 - 2 * s)))

        def second1(self):
            self.m1 = []
            for s in (0, 1):
                b = 1 - 2 * s
                xi, yi = self.at(0, b)
                o, n = self.h[s]
                total = self.sum1(b)
                self.m0[s].wait_recv()
                other = slice(n, None) if o == 0 else slice(0, o)
                self.ref[xi, yi, pl.ds(o, n)] = (
                    total[o:o + n] + self.q0[s, pl.ds(0, n)].astype(F32)).astype(BF16)
                so, sn = self.h[1 - s]
                self.ref[xi, yi, pl.ds(so, sn)] = total[other].astype(BF16)
                self.m1.append(msg.start(self.ref.at[xi, yi], self.q1.at[s], dev(self.b, b)))

        def result(self):
            total = self.sum1(0)
            for s in (0, 1):
                self.m1[s].wait_recv()
            return total + self.q1[0].astype(F32) + self.q1[1].astype(F32)

    rb = Reduce(br, "y", "x", HALF, b0, b1, bq0, bq1)
    rd = Reduce(dn, "x", "y", HALFE, d0, d1, dq0, dq1)

    def branch_block(off):
        xi = px(off)
        val = dot(w[1, rows(xi, DX)], hd[1], 1, 0).astype(BF16)
        for j in range(NY):
            br[xi, j] = val[:, j * TB:(j + 1) * TB]

    def normed_block(off):
        xi = px(off)
        val = dot(w[0, rows(xi, DX)], hd[0], 1, 0).astype(BF16)
        for j in range(NY):
            dn[xi, j, pl.ds(0, DX)] = val[:, j * TB:(j + 1) * TB]
            dn[xi, j, pl.ds(DX, EX)] = jnp.broadcast_to(
                md_s[:, j * TB:(j + 1) * TB], (EX, TB)).astype(BF16)

    grad_chunk(0)
    branch_block(2)
    rb.send0(2)
    normed_block(2)
    for b in ORDER:
        rd.send0(b)
    fold(0)
    z_reduce(0, 0, 0)
    z_reduce(0, 0, 1)
    grad_chunk(1)
    grad_chunk(2)
    branch_block(1)
    rb.send0(1)
    branch_block(-1)
    rb.send0(-1)
    fold(1)
    fold(2)
    branch_block(0)
    rb.send0(0)
    normed_block(1)
    normed_block(-1)
    z_reduce(1, 1, 0)
    z_reduce(1, 2, 1)
    rb.send1(2)
    rd.send1(2)
    grad_chunk(3)
    grad_chunk(4)
    normed_block(0)
    for b in (1, -1, 0):
        rb.send1(b)
        rd.send1(b)
    fold(3)
    fold(4)
    z_reduce(2, 3, 0)
    z_reduce(2, 4, 1)
    for k in (5, 6, 7):
        grad_chunk(k)
    rb.second0()
    rd.second0()
    for k in (5, 6, 7):
        fold(k)
    gain = gain_x()
    z_reduce(3, 5, 0)
    z_reduce(3, 6, 1)
    gain = gain_y(gain)
    rb.second1()
    gain = gain_z(gain)
    rd.second1()
    gain = gain_ring(gain, 1)

    xf = xo[...].astype(F32)
    out_ref[...] = (xf + rb.result()).astype(BF16)
    stores = [pltpu.make_async_copy(out_ref, out_hbm, copy_sem.at[0])]
    stores[0].start()
    gain = gain_ring(gain, 2)
    total = rd.result()
    dnorm = total[:DX]
    inv = inv_s[...]
    mean_dot = total[DX:DX + 1] / D
    unit = xf * inv
    dtok_ref[...] = (
        co[...].astype(F32) + inv * (dnorm * gcol[x] - unit * mean_dot)
    ).astype(BF16)
    stores.append(pltpu.make_async_copy(dtok_ref, dtok_hbm, copy_sem.at[1]))
    stores[1].start()
    gain = gain_ring(gain, 3)

    for p in (0, 1):
        for sub in (0, 1):
            zmsg[p, 3, sub].wait_recv()
    final = g[7] + zr[0, 3].astype(F32) + zr[1, 3].astype(F32)
    final = jnp.concatenate([final[:DZ], tail_of(final)], axis=1).astype(BF16)
    stage[...] = dot(select, final, 0, 0).astype(BF16).reshape(NY, RP, FP)
    back = [msg.start(stage.at[py(off)], ga.at[d, y], dev("y", off)) for off in (1, -1, 2)]
    ga[d, y] = stage[y]
    hands = [msg.start(ga.at[d, y], ga.at[d, y], dev("c"))]
    gain = gain_c(gain)
    for cp, off in zip(back, (1, -1, 2)):
        cp.wait_recv()
        ref = ga.at[d, py(-off)]
        hands.append(msg.start(ref, ref, dev("c")))
    for cp in hands:
        cp.wait_recv()
    for i, ref in enumerate((gu_ref, gd_ref)):
        for j in range(NY):
            ref[:, pl.ds(j * FS, FS)] = ga[i, j][:DC, :FS]
    for i, (ref, hbm) in enumerate(((gu_ref, gu_hbm), (gd_ref, gd_hbm))):
        stores.append(pltpu.make_async_copy(ref, hbm, copy_sem.at[2 + i]))
        stores[2 + i].start()
    for cp in gain:
        cp.wait_recv()
    total = jnp.where(d == 0, ggc[0], ggc[1]) * SCALE
    for i in (0, 1):
        row = jnp.concatenate([total[4 * i + j:4 * i + j + 1] for j in range(4)], axis=1)
        gg_ref[:, pl.ds(i * DZ, DZ)] = row[:, :DZ]
    gg_ref[...] = gg_ref[...] / gain_own
    msg.drain()
    for cp in stores:
        cp.wait()


def vm(shape, dtype=BF16):
    return pltpu.VMEM(shape, dtype)


def block(x, c, up, down, g):
    spec = pl.BlockSpec(memory_space=pltpu.VMEM)
    anywhere = pl.BlockSpec(memory_space=pl.ANY)
    return pl.pallas_call(
        kernel,
        out_shape=(
            jax.ShapeDtypeStruct((DX, TB), BF16),
            jax.ShapeDtypeStruct((DX, TB), BF16),
            jax.ShapeDtypeStruct((DC, NY * FS), BF16),
            jax.ShapeDtypeStruct((DC, NY * FS), BF16),
            jax.ShapeDtypeStruct((1, DX), F32),
        ),
        in_specs=[anywhere] * 4 + [spec],
        out_specs=(anywhere,) * 4 + (spec,),
        scratch_shapes=[
            vm((DX, TB)),
            vm((DX, TB)),
            vm((DC, NY * FS)),
            vm((NY, RP, FP)),
            vm((NZ, ZP, FM)),
            vm((DX, TB)),
            vm((DX, TB)),
            vm((DC, NY * FS)),
            vm((DC, NY * FS)),
            vm((D, T)),
            vm((2, D, T)),
            vm((2, D, FP)),
            vm((NY, RP, FP)),
            vm((NX, 8, 896), F32),
            vm((NX, DX, TB), F32),
            vm((1, TB), F32),
            vm((FP, T), F32),
            vm((FP, T), F32),
            vm((2, FP, T)),
            vm((1, T), F32),
            vm((NZ, DZ, FP), F32),
            vm((NZ, ZP, FM), F32),
            vm((NZ, DZ, FP)),
            vm((2, 4, ZP, FM)),
            vm((2, 4, ZP, FM)),
            vm((NX, NY, DX, TB)),
            vm((NX, NY, DE, TB)),
            vm((4, 2, 400, TB)),
            vm((4, 2, DX, TB)),
            vm((2, 400, TB)),
            vm((2, DX, TB)),
            vm((4, 2, 416, TB)),
            vm((4, 2, DE, TB)),
            vm((2, 416, TB)),
            vm((2, DE, TB)),
            vm((NY, RP, FP)),
            vm((2, NY, RP, FP)),
            vm((NX, 8, TB), F32),
            vm((8, FP), F32),
            vm((3, 8, TB), F32),
            vm((4, 8, TB), F32),
            vm((NZ, 8, TB), F32),
            vm((2, 8, TB), F32),
            pltpu.SemaphoreType.DMA((N_MESSAGES,)),
            pltpu.SemaphoreType.DMA((N_MESSAGES,)),
            pltpu.SemaphoreType.DMA((4,)),
        ],
        compiler_params=pltpu.CompilerParams(
            collective_id=0, has_side_effects=True, vmem_limit_bytes=60 * 2**20
        ),
    )(x, c, up, down, g)


def on_device(tokens, gain, w_up, w_down, cotangent):
    out, d_tokens, grad_up, grad_down, grad_gain = block(
        tokens.T, cotangent.T, w_up, w_down.T, gain.reshape(1, DX))
    return (
        out.T, d_tokens.T, grad_up.astype(F32) * SCALE, grad_down.T.astype(F32) * SCALE,
        grad_gain.reshape(DX),
    )


def solution(mesh):
    in_specs = (
        P(("depth", "col"), "row"),
        P("row"),
        P("col", "row"),
        P("row", "col"),
        P(("depth", "col"), "row"),
    )
    out_specs = (
        P(("depth", "col"), "row"),
        P(("depth", "col"), "row"),
        P("col", "row"),
        P("row", "col"),
        P("row"),
    )
    return jax.shard_map(
        on_device, mesh=mesh, in_specs=in_specs, out_specs=out_specs, check_vma=False
    )
```

```python
import math

import jax
import jax.numpy as jnp
from jax import lax
from jax.experimental import pallas as pl
from jax.experimental.pallas import tpu as pltpu
from jax.sharding import PartitionSpec as P

EPS = 1e-06
MESH = pl.DeviceIdType.MESH
F32, BF16 = jnp.float32, jnp.bfloat16

NX, NY, NZ = 4, 4, 8
D, FF, TOK = 3200, 6400, 8192
DX = D // NX
TB = 128
T = NY * TB
DZ = D // NZ
DC = D // (NY * NZ)
FS = FF // (NX * NY)
FP = 512
RP = 112
EX = 16
DE = DX + EX
FM = 384
ZP = 432
SUBS = ((0, 208), (208, 224))
HALF = ((0, 400), (400, 400))
HALFE = ((0, 400), (400, 416))
ORDER = (2, 1, -1, 0)
ZORDER = (4, 3, -3, 2, -2, 1, -1, 0)
SCALE = TOK ** (-0.5)


def gelu_value(pre):
    return 0.5 * pre * (1.0 + lax.erf(pre / math.sqrt(2.0)))


def gelu_slope(pre):
    return 0.5 * (1.0 + lax.erf(pre / math.sqrt(2.0))) + pre * jnp.exp(
        -0.5 * pre * pre
    ) / math.sqrt(2.0 * math.pi)


def dot(left, right, left_dim, right_dim):
    return lax.dot_general(
        left, right, (((left_dim,), (right_dim,)), ((), ())), preferred_element_type=F32
    )


class Messages:
    def __init__(self, send, recv):
        self.send, self.recv, self.n, self.live = send, recv, 0, []

    def start(self, src, dst, device):
        i = self.n
        self.n += 1
        cp = pltpu.make_async_remote_copy(
            src_ref=src, dst_ref=dst, send_sem=self.send.at[i], recv_sem=self.recv.at[i],
            device_id=device, device_id_type=MESH,
        )
        cp.start()
        self.live.append(cp)
        return cp

    def drain(self):
        for cp in self.live:
            cp.wait_send()
        self.live = []


N_MESSAGES = 224

SCHEDULE = (
    ("B", 2), ("N", 2), ("G", 0), ("b0", 2), ("N", 1), ("B", 1), ("b0", 1), ("B", -1), ("N", -1), ("b0", -1),
    ("d0", 2), ("G", 1), ("F", 0), ("Z", 0, 0, 0), ("Z", 0, 1, 1), ("Z", 0, 0, 2), ("G", 2), ("b1", 2, 0),
    ("b1", 2, 1), ("B", 0), ("G", 3), ("G", 4), ("b1", 1, 1), ("d1", 2, 0), ("d1", 2, 1), ("Z", 0, 1, 3), ("F", 1),
    ("F", 2), ("Z", 1, 1, 0), ("Z", 1, 0, 0), ("Z", 1, 1, 1), ("Z", 1, 0, 1), ("G", 7), ("b1", -1, 1), ("b1", -1, 0),
    ("G", 5), ("Z", 1, 0, 2), ("b1", 1, 0), ("Z", 1, 1, 2), ("d0", -1), ("F", 3), ("b0", 0), ("N", 0), ("G", 6),
    ("Z", 2, 0, 0), ("F", 4), ("Z", 1, 1, 3), ("d0", 1), ("Z", 1, 0, 3), ("F", 7), ("Z", 2, 1, 0), ("P", 3), ("F", 5),
    ("Z", 2, 0, 1), ("P", 1), ("P", 7), ("P", 5), ("F", 6), ("Z", 2, 1, 1), ("P", 0), ("d1", -1, 0), ("d1", -1, 1),
    ("Z", 2, 0, 2), ("P", 2), ("P", 6), ("Z", 2, 1, 2), ("P", 4), ("g", 0), ("d2",), ("Z", 3, 0, 0), ("d0", 0),
    ("b2",), ("d1", 1, 1), ("d1", 1, 0), ("Z", 2, 1, 3), ("Z", 2, 0, 3), ("Z", 3, 1, 0), ("Z", 3, 0, 1),
    ("Z", 3, 1, 1), ("g", 1), ("Z", 3, 0, 2), ("Z", 3, 1, 2), ("b1", 0, 0), ("b1", 0, 1), ("d1", 0, 1), ("d1", 0, 0),
    ("Z", 3, 1, 3), ("Z", 3, 0, 3), ("d3", 1), ("g", 2), ("b3", 1), ("b3", 0), ("ZF", 0), ("ZF", 1), ("ZF", 2),
    ("d3", 0), ("g", 3), ("ZF", 3), ("g", 4), ("H", 0), ("g", 5), ("H", 1), ("H", 2), ("AO",), ("g", 6), ("AE",),
    ("RB",), ("RD",),
)


def kernel(
    x_in, c_in, up_in, down_in, g_in,
    out_hbm, dtok_hbm, gu_hbm, gd_hbm, gg_ref,
    xo, co, ws, w_in, wz, out_ref, dtok_ref, go, xt, nc, w, wa, gr, gcol, inv_s, pre_s, dh_s, hd, md_s, gs, g, xr, zs, zr,
    br, dn, b0, b1, bq0, bq1, d0, d1, dq0, dq1, stage, ga, ggp, ggr, ggx, ggy, ggz, ggc,
    send_sem, recv_sem, copy_sem,
):
    x = lax.axis_index("row")
    col = lax.axis_index("col")
    d = lax.axis_index("depth")
    y, z = lax.rem(col, NY), col // NY
    e = 1 - d

    def dev(ax=None, off=0):
        xx, yy, zz, dd = x, y, z, d
        if ax == "x":
            xx = lax.rem(x + (off + NX), NX)
        elif ax == "y":
            yy = lax.rem(y + (off + NY), NY)
        elif ax == "z":
            zz = lax.rem(z + (off + NZ), NZ)
        elif ax == "c":
            dd = e
        return (xx, zz * NY + yy, dd)

    def px(off):
        return lax.rem(x + (off + NX), NX)

    def py(off):
        return lax.rem(y + (off + NY), NY)

    def pz(off):
        return lax.rem(z + (off + NZ), NZ)

    def rows(i, size, off=0, n=None):
        return pl.ds(pl.multiple_of(i * size + off, 16), size if n is None else n)

    def lanes(i):
        return pl.ds(pl.multiple_of(i * TB, TB), TB)

    msg = Messages(send_sem, recv_sem)

    barrier = pltpu.get_barrier_semaphore()
    partners = [("x", 1), ("x", -1), ("x", 2), ("y", 1), ("y", -1), ("y", 2), ("z", 1), ("z", -1), ("c", 0)]
    for ax, off in partners:
        pl.semaphore_signal(barrier, inc=1, device_id=dev(ax, off), device_id_type=MESH)

    loads = [pltpu.make_async_copy(x_in, xo, copy_sem.at[0]), pltpu.make_async_copy(c_in, co, copy_sem.at[1])]
    for cp in loads:
        cp.start()

    @pl.when(d == 0)
    def _():
        cp = pltpu.make_async_copy(up_in, ws, copy_sem.at[2])
        cp.start()
        cp.wait()

    @pl.when(d == 1)
    def _():
        cp = pltpu.make_async_copy(down_in, ws, copy_sem.at[2])
        cp.start()
        cp.wait()

    w_in[...] = jnp.zeros_like(w_in)
    for j in range(NY):
        w_in[j, pl.ds(0, DC), pl.ds(0, FS)] = ws[:, j * FS:(j + 1) * FS]
    for cp in loads:
        cp.wait()
    xt[rows(x, DX), lanes(y)] = xo[...]
    nc[1, rows(x, DX), lanes(y)] = co[...]
    gain_own = g_in[...].astype(F32)
    gr[x] = jnp.zeros_like(gr[0])
    gr[x, :, pl.ds(0, DX)] = jnp.broadcast_to(gain_own, (8, DX))
    pl.semaphore_wait(barrier, len(partners))

    class Gather:
        def __init__(self, ref, first, second):
            self.ref, self.a, self.b = ref, first, second
            self.n1, self.n2 = {}, {}

        def at(self, a, b, half=None):
            xi, yi = (px(a), py(b)) if self.a == "x" else (px(b), py(a))
            off, n = (0, DX) if half is None else HALF[half]
            return self.ref(rows(xi, DX, off, n), lanes(yi))

        def go(self, a, b, ax, off, half=None):
            ref = self.at(a, b, half)
            return msg.start(ref, ref, dev(ax, off))

        def first(self):
            self.m1 = [self.go(0, 0, self.a, 1), self.go(0, 0, self.a, -1)]

        def second(self, a):
            self.n1[a] = [self.go(a, 0, self.b, 1), self.go(a, 0, self.b, -1)]

        def first_forward(self):
            self.m1[0].wait_recv()
            m2p = self.go(-1, 0, self.a, 1, 0)
            self.m1[1].wait_recv()
            m2m = self.go(1, 0, self.a, -1, 1)
            self.m2 = [m2p, m2m]

        def first_done(self):
            for cp in self.m2:
                cp.wait_recv()

        def second_forward(self, a):
            self.n1[a][0].wait_recv()
            p = self.go(a, -1, self.b, 1, 0)
            self.n1[a][1].wait_recv()
            m = self.go(a, 1, self.b, -1, 1)
            self.n2[a] = [p, m]

        def second_done(self, a):
            for cp in self.n2[a]:
                cp.wait_recv()

    gx = Gather(lambda r, l: xt.at[r, l], "x", "y")
    gc = Gather(lambda r, l: nc.at[1, r, l], "y", "x")

    gain_msgs = [msg.start(gr.at[x], gr.at[x], dev("x", off)) for off in (1, -1, 2)]
    a2a = [msg.start(w_in.at[py(off)], wa.at[y], dev("y", off)) for off in (1, -1, 2)]
    gx.first()
    gc.first()
    gx.second(0)
    gc.second(0)
    wa[y] = w_in[y]

    r_i = lax.broadcasted_iota(jnp.int32, (DZ, NY * RP), 0)
    c_i = lax.broadcasted_iota(jnp.int32, (DZ, NY * RP), 1)
    shift = jnp.where(r_i >= 3 * DC, 3, jnp.where(r_i >= 2 * DC, 2, jnp.where(r_i >= DC, 1, 0)))
    select = jnp.where(c_i == r_i + (RP - DC) * shift, 1.0, 0.0).astype(BF16)

    for cp in a2a:
        cp.wait_recv()
    own = dot(select, wa[...].reshape(NY * RP, FP), 1, 0)
    w[d, rows(z, DZ)] = own.astype(BF16)

    def pack(ref, i, val):
        tail = jnp.concatenate([val[:, FM:], jnp.zeros((FP - DZ, FP - FM), F32)], axis=0).T[:16]
        ref[i, pl.ds(0, DZ)] = val[:, :FM].astype(ref.dtype)
        ref[i, pl.ds(DZ, 16)] = tail[:, :FM].astype(ref.dtype)
        ref[i, pl.ds(DZ + 16, 16), pl.ds(0, FP - FM)] = tail[:, FM:].astype(ref.dtype)

    def tail_of(val):
        tail = jnp.concatenate([val[DZ:DZ + 16], val[DZ + 16:, :FP - FM]], axis=1)
        tail = jnp.concatenate([tail, jnp.zeros((FP - FM - 16, FP), F32)], axis=0)
        return tail.T[:DZ]

    wz[z, pl.ds(DZ + 16, 16), :] = jnp.zeros((16, FM), BF16)
    pack(wz, z, own)

    def pack_parts(k, val):
        tail = jnp.concatenate([val[:, FM:], jnp.zeros((FP - DZ, FP - FM), F32)], axis=0).T[:16]
        for q in range(NY):
            g[k, q, pl.ds(0, DC)] = val[q * DC:(q + 1) * DC, :FM]
            for i in (0, 1):
                g[k, q, pl.ds(RP - 8, 8), pl.ds(i * TB, TB)] = tail[i * 8:i * 8 + 8, q * DC:q * DC + TB]

    def unpack_part(val):
        tail = jnp.concatenate([val[RP - 8:, :TB], val[RP - 8:, TB:2 * TB], jnp.zeros((TB - 16, TB), F32)], axis=0)
        return jnp.concatenate([val[:DC], tail.T[:DC, :16]], axis=1)

    def w_at(off, sub):
        o, n = SUBS[sub]
        return wz.at[pz(off), pl.ds(o, n)]

    def hand(off):
        ref = w.at[d, rows(pz(off), DZ)]
        wc.append(msg.start(ref, ref, dev("c")))

    def unpack(off):
        r = rows(pz(off), DZ)
        w[d, r, pl.ds(0, FM)] = wz[pz(off), pl.ds(0, DZ)]
        w[d, r, pl.ds(FM, FP - FM)] = tail_of(wz[pz(off)].astype(F32)).astype(BF16)
        hand(off)

    zp, zm, wc = {}, {}, []

    def z_send(s):
        for sub in (0, 1):
            if s < 3 or sub == 0:
                zp[s, sub] = msg.start(w_at(-s, sub), w_at(-s, sub), dev("z", 1))
            if s < 3 or sub == 1:
                zm[s, sub] = msg.start(w_at(s, sub), w_at(s, sub), dev("z", -1))

    def z_step(s):
        for sub in (0, 1):
            if (s, sub) in zp:
                zp[s, sub].wait_recv()
                if s < 2 or (s == 2 and sub == 0):
                    ref = w_at(-(s + 1), sub)
                    zp[s + 1, sub] = msg.start(ref, ref, dev("z", 1))
            if (s, sub) in zm:
                zm[s, sub].wait_recv()
                if s < 2 or (s == 2 and sub == 1):
                    ref = w_at(s + 1, sub)
                    zm[s + 1, sub] = msg.start(ref, ref, dev("z", -1))
        unpack(s + 1)
        if s < 3:
            unpack(-(s + 1))

    z_send(0)
    hand(0)

    gx.first_forward()
    gc.first_forward()
    for a in (-1, 1):
        gx.second(a)
        gc.second(a)
    for cp in gain_msgs:
        cp.wait_recv()

    def spread_gain(i, carry):
        column = gr[i].T[:DX, 0:1]
        gcol[i] = jnp.broadcast_to(column, (DX, TB))
        return carry

    lax.fori_loop(0, NX, spread_gain, 0)

    def normalise(off):
        yi = py(off)

        def square(i, acc):
            v = xt[pl.ds(pl.multiple_of(i * 160, 16), 160), lanes(yi)].astype(F32)
            return acc + jnp.sum(v * v, axis=0, keepdims=True)

        total = lax.fori_loop(0, D // 160, square, jnp.zeros((1, TB), F32))
        inv = lax.rsqrt(total / D + EPS)
        if off == 0:
            inv_s[...] = inv

        def scale(i, carry):
            xi, k = i // 5, lax.rem(i, 5)
            r = pl.ds(pl.multiple_of(i * 160, 16), 160)
            v = xt[r, lanes(yi)].astype(F32) * inv
            nc[0, r, lanes(yi)] = (v * gcol[xi, pl.ds(pl.multiple_of(k * 160, 16), 160)]).astype(BF16)
            return carry

        lax.fori_loop(0, D // 160, scale, 0)

    gx.first_done()
    gx.second(2)
    gc.first_done()
    gc.second(2)
    normalise(0)
    gx.second_forward(0)
    gc.second_forward(0)
    z_step(0)
    for a in (-1, 1):
        gx.second_forward(a)
        gc.second_forward(a)
    z_step(1)
    gx.second_forward(2)
    gc.second_forward(2)
    normalise(1)
    normalise(-1)
    z_step(2)
    for a in (0, -1, 1, 2):
        gx.second_done(a)
    normalise(2)
    for a in (0, -1, 1, 2):
        gc.second_done(a)
    z_step(3)
    for cp in wc:
        cp.wait_recv()
    msg.drain()

    pre_s[...] = jnp.zeros_like(pre_s)
    dh_s[...] = jnp.zeros_like(dh_s)

    def up(i, carry):
        r = rows(i, DZ)
        pre_s[...] += dot(w[0, r], nc[0, r], 0, 0)
        dh_s[...] += dot(w[1, r], nc[1, r], 0, 0)
        return carry

    lax.fori_loop(0, NZ, up, 0)

    hd[0, pl.ds(FS, FP - FS)] = jnp.zeros((FP - FS, T), BF16)
    hd[1, pl.ds(FS, FP - FS)] = jnp.zeros((FP - FS, T), BF16)

    def act(i, acc):
        r = pl.ds(pl.multiple_of(i * 16, 16), 16)
        pre = pre_s[r]
        dpre = dh_s[r] * gelu_slope(pre)
        hd[1, r] = gelu_value(pre).astype(BF16)
        hd[0, r] = dpre.astype(BF16)
        return acc + jnp.sum(dpre * pre, axis=0, keepdims=True)

    md_s[...] = lax.fori_loop(0, FS // 16, act, jnp.zeros((1, T), F32))

    core = {}
    ggr[...] = jnp.zeros_like(ggr)
    g[...] = jnp.zeros_like(g)
    ones = jnp.ones((8, FP), BF16)

    def fold(k):
        core[k].wait_recv()
        total = gs[k] + xr[k].astype(F32)
        pack_parts(k, total)
        gs[k] = total

    def gain_part(k):
        zc = pz(ZORDER[k])
        v = gs[k] * w[d, rows(zc, DZ)].astype(F32)
        high = v.astype(BF16)
        low = (v - high.astype(F32)).astype(BF16)
        ggr[:, pl.ds(0, DZ)] = dot(ones, high, 1, 1) + dot(ones, low, 1, 1)
        for j in range(4):
            ggp[zc // 2, pl.ds(lax.rem(zc, 2) * 4 + j, 1), :] = ggr[0:1, j * TB:(j + 1) * TB]

    def gain_x():
        return [msg.start(ggp.at[px(off)], ggx.at[i], dev("x", off)) for i, off in enumerate((1, -1, 2))]

    def gain_y(cps):
        for cp in cps:
            cp.wait_recv()
        ggy[0] = ggp[x] + ggx[0] + ggx[1] + ggx[2]
        return [msg.start(ggy.at[0], ggy.at[1 + i], dev("y", off)) for i, off in enumerate((1, -1, 2))]

    def gain_z(cps):
        for cp in cps:
            cp.wait_recv()
        ggz[0] = ggy[0] + ggy[1] + ggy[2] + ggy[3]
        return [msg.start(ggz.at[0], ggz.at[1 + p], dev("z", 1 - 2 * p)) for p in (0, 1)]

    def gain_ring(cps, s):
        for cp in cps:
            cp.wait_recv()
        return [
            msg.start(ggz.at[2 * s - 1 + p], ggz.at[2 * s + 1 + p], dev("z", 1 - 2 * p))
            for p in ((0, 1) if s < 3 else (0,))
        ]

    def gain_c(cps):
        for cp in cps:
            cp.wait_recv()
        total = ggz[0]
        for i in range(NZ - 1):
            total = total + ggz[1 + i]
        ggc[0] = total
        return [msg.start(ggc.at[0], ggc.at[1], dev("c"))]

    def grad_chunk(k):
        r = rows(pz(ZORDER[k]), DZ)
        xt[pl.ds(k * DZ, DZ)] = dot(nc[e, r], hd[e], 1, 1).astype(BF16)
        core[k] = msg.start(xt.at[pl.ds(k * DZ, DZ)], xr.at[k], dev("c"))
        gs[k] = dot(nc[d, r], hd[d], 1, 1)

    zmsg = {}

    def z_reduce(s, p, j):
        k = 0 if s == 0 else 2 * s - 1 + p
        q = py(ORDER[j])
        val = g[k, q]
        if (s - 1, p, j) in zmsg:
            zmsg[s - 1, p, j].wait_recv()
            val = val + zr[p, s - 1, q].astype(F32)
        zs[p, s, q] = val.astype(BF16)
        zmsg[s, p, j] = msg.start(zs.at[p, s, q], zr.at[p, s, q], dev("z", 1 - 2 * p))

    back, hands = {}, {}

    def z_final(j):
        q = py(ORDER[j])
        for p in (0, 1):
            zmsg[3, p, j].wait_recv()
        val = (g[7, q] + zr[0, 3, q].astype(F32) + zr[1, 3, q].astype(F32)).astype(BF16)
        if j < 3:
            stage[j] = val
            back[j] = msg.start(stage.at[j], ga.at[d, y], dev("y", ORDER[j]))
        else:
            ga[d, y] = val
            hands[j] = msg.start(ga.at[d, y], ga.at[d, y], dev("c"))

    def hand_on(j):
        back[j].wait_recv()
        ref = ga.at[d, py(-ORDER[j])]
        hands[j] = msg.start(ref, ref, dev("c"))

    def assemble(i):
        for j in range(NY):
            go[i, :, pl.ds(j * FS, FS)] = unpack_part(ga[i, j].astype(F32)).astype(BF16)

    class Reduce:
        def __init__(self, ref, a, b, halves, r0, r1, q0, q1):
            self.ref, self.a, self.b, self.h = ref, a, b, halves
            self.r0, self.r1, self.q0, self.q1 = r0, r1, q0, q1
            self.p0, self.p1, self.m1 = {}, {}, {}

        def at(self, a, b):
            return (px(a), py(b)) if self.a == "x" else (px(b), py(a))

        def send0(self, b):
            i = ORDER.index(b)
            xi, yi = self.at(2, b)
            self.p0[b] = []
            for s in (0, 1):
                o, n = self.h[s]
                self.p0[b].append(msg.start(
                    self.ref.at[xi, yi, pl.ds(o, n)], self.r0.at[i, s, pl.ds(0, n)], dev(self.a, 1 - 2 * s)))

        def send1(self, b, s):
            i = ORDER.index(b)
            o, n = self.h[s]
            xi, yi = self.at(1 - 2 * s, b)
            self.p0[b][s].wait_recv()
            self.ref[xi, yi, pl.ds(o, n)] = (
                self.ref[xi, yi, pl.ds(o, n)].astype(F32) + self.r0[i, s, pl.ds(0, n)].astype(F32)
            ).astype(BF16)
            self.p1[b, s] = msg.start(self.ref.at[xi, yi], self.r1.at[i, s], dev(self.a, 1 - 2 * s))

        def sum1(self, b):
            i = ORDER.index(b)
            xi, yi = self.at(0, b)
            for s in (0, 1):
                self.p1[b, s].wait_recv()
            return self.ref[xi, yi].astype(F32) + self.r1[i, 0].astype(F32) + self.r1[i, 1].astype(F32)

        def second0(self):
            xi, yi = self.at(0, 2)
            self.ref[xi, yi] = self.sum1(2).astype(BF16)
            self.m0 = []
            for s in (0, 1):
                o, n = self.h[s]
                self.m0.append(msg.start(
                    self.ref.at[xi, yi, pl.ds(o, n)], self.q0.at[s, pl.ds(0, n)], dev(self.b, 1 - 2 * s)))

        def second1(self, s):
            b = 1 - 2 * s
            xi, yi = self.at(0, b)
            o, n = self.h[s]
            total = self.sum1(b)
            self.m0[s].wait_recv()
            self.ref[xi, yi, pl.ds(o, n)] = (
                total[o:o + n] + self.q0[s, pl.ds(0, n)].astype(F32)).astype(BF16)
            so, sn = self.h[1 - s]
            self.ref[xi, yi, pl.ds(so, sn)] = total[so:so + sn].astype(BF16)
            self.m1[s] = msg.start(self.ref.at[xi, yi], self.q1.at[s], dev(self.b, b))

        def result(self):
            total = self.sum1(0)
            for s in (0, 1):
                self.m1[s].wait_recv()
            return total + self.q1[0].astype(F32) + self.q1[1].astype(F32)

    rb = Reduce(br, "y", "x", HALF, b0, b1, bq0, bq1)
    rd = Reduce(dn, "x", "y", HALFE, d0, d1, dq0, dq1)

    def branch_block(off):
        xi = px(off)
        val = dot(w[1, rows(xi, DX)], hd[1], 1, 0).astype(BF16)
        for j in range(NY):
            br[xi, j] = val[:, j * TB:(j + 1) * TB]

    def normed_block(off):
        xi = px(off)
        val = dot(w[0, rows(xi, DX)], hd[0], 1, 0).astype(BF16)
        for j in range(NY):
            dn[xi, j, pl.ds(0, DX)] = val[:, j * TB:(j + 1) * TB]
            dn[xi, j, pl.ds(DX, EX)] = jnp.broadcast_to(
                md_s[:, j * TB:(j + 1) * TB], (EX, TB)).astype(BF16)

    def out_result():
        out_ref[...] = (xo[...].astype(F32) + rb.result()).astype(BF16)
        stores[0].start()

    def dtok_result():
        total = rd.result()
        dnorm = total[:DX]
        inv = inv_s[...]
        mean_dot = total[DX:DX + 1] / D
        unit = xo[...].astype(F32) * inv
        dtok_ref[...] = (
            co[...].astype(F32) + inv * (dnorm * gcol[x] - unit * mean_dot)
        ).astype(BF16)
        stores[1].start()

    chain = [gain_x, gain_y, gain_z, lambda m: gain_ring(m, 1), lambda m: gain_ring(m, 2),
             lambda m: gain_ring(m, 3), gain_c]
    gain = None

    def gain_step(i):
        nonlocal gain
        gain = chain[i](gain) if i else chain[0]()

    stores = [
        pltpu.make_async_copy(src, dst, copy_sem.at[i])
        for i, (src, dst) in enumerate((
            (out_ref, out_hbm), (dtok_ref, dtok_hbm), (go.at[0], gu_hbm), (go.at[1], gd_hbm)))
    ]

    def other_core():
        for j in range(NY):
            hands[j].wait_recv()
        assemble(e)

    steps = {
        "B": branch_block, "N": normed_block, "G": grad_chunk, "F": fold, "P": gain_part,
        "Z": z_reduce, "ZF": z_final, "H": hand_on, "AO": lambda: assemble(d), "AE": other_core,
        "b0": rb.send0, "b1": rb.send1, "b2": rb.second0, "b3": rb.second1, "RB": out_result,
        "d0": rd.send0, "d1": rd.send1, "d2": rd.second0, "d3": rd.second1, "RD": dtok_result,
        "g": gain_step,
    }
    for name, *where in SCHEDULE:
        steps[name](*where)

    for i in (2, 3):
        stores[i].start()
    for cp in gain:
        cp.wait_recv()
    total = jnp.where(d == 0, ggc[0], ggc[1]) * SCALE
    for i in (0, 1):
        row = jnp.concatenate([total[4 * i + j:4 * i + j + 1] for j in range(4)], axis=1)
        gg_ref[:, pl.ds(i * DZ, DZ)] = row[:, :DZ]
    gg_ref[...] = gg_ref[...] / gain_own
    msg.drain()
    for cp in stores:
        cp.wait()


def vm(shape, dtype=BF16):
    return pltpu.VMEM(shape, dtype)


def block(x, c, up, down, g):
    spec = pl.BlockSpec(memory_space=pltpu.VMEM)
    anywhere = pl.BlockSpec(memory_space=pl.ANY)
    return pl.pallas_call(
        kernel,
        out_shape=(
            jax.ShapeDtypeStruct((DX, TB), BF16),
            jax.ShapeDtypeStruct((DX, TB), BF16),
            jax.ShapeDtypeStruct((DC, NY * FS), BF16),
            jax.ShapeDtypeStruct((DC, NY * FS), BF16),
            jax.ShapeDtypeStruct((1, DX), F32),
        ),
        in_specs=[anywhere] * 4 + [spec],
        out_specs=(anywhere,) * 4 + (spec,),
        scratch_shapes=[
            vm((DX, TB)),
            vm((DX, TB)),
            vm((DC, NY * FS)),
            vm((NY, RP, FP)),
            vm((NZ, ZP, FM)),
            vm((DX, TB)),
            vm((DX, TB)),
            vm((2, DC, NY * FS)),
            vm((D, T)),
            vm((2, D, T)),
            vm((2, D, FP)),
            vm((NY, RP, FP)),
            vm((NX, 8, 896), F32),
            vm((NX, DX, TB), F32),
            vm((1, TB), F32),
            vm((FP, T), F32),
            vm((FP, T), F32),
            vm((2, FP, T)),
            vm((1, T), F32),
            vm((NZ, DZ, FP), F32),
            vm((NZ, NY, RP, FM), F32),
            vm((NZ, DZ, FP)),
            vm((2, 4, NY, RP, FM)),
            vm((2, 4, NY, RP, FM)),
            vm((NX, NY, DX, TB)),
            vm((NX, NY, DE, TB)),
            vm((4, 2, 400, TB)),
            vm((4, 2, DX, TB)),
            vm((2, 400, TB)),
            vm((2, DX, TB)),
            vm((4, 2, 416, TB)),
            vm((4, 2, DE, TB)),
            vm((2, 416, TB)),
            vm((2, DE, TB)),
            vm((3, RP, FM)),
            vm((2, NY, RP, FM)),
            vm((NX, 8, TB), F32),
            vm((8, FP), F32),
            vm((3, 8, TB), F32),
            vm((4, 8, TB), F32),
            vm((NZ, 8, TB), F32),
            vm((2, 8, TB), F32),
            pltpu.SemaphoreType.DMA((N_MESSAGES,)),
            pltpu.SemaphoreType.DMA((N_MESSAGES,)),
            pltpu.SemaphoreType.DMA((4,)),
        ],
        compiler_params=pltpu.CompilerParams(
            collective_id=0, has_side_effects=True, vmem_limit_bytes=60 * 2**20
        ),
    )(x, c, up, down, g)


def finish(out_in, dtok_in, gu_in, gd_in, gg_in, out_ref, dtok_ref, gu_ref, gd_ref, gg_ref):
    out_ref[...] = out_in[...]
    dtok_ref[...] = dtok_in[...]
    gu_ref[...] = gu_in[...].astype(F32) * SCALE
    gd_ref[...] = gd_in[...].astype(F32) * SCALE
    gg_ref[...] = gg_in[...]


def on_device(tokens, gain, w_up, w_down, cotangent):
    parts = block(tokens.T, cotangent.T, w_up, w_down.T, gain.reshape(1, DX))
    spec = pl.BlockSpec(memory_space=pltpu.VMEM)
    out, d_tokens, grad_up, grad_down, grad_gain = pl.pallas_call(
        finish,
        out_shape=(
            jax.ShapeDtypeStruct((DX, TB), BF16),
            jax.ShapeDtypeStruct((DX, TB), BF16),
            jax.ShapeDtypeStruct((DC, NY * FS), F32),
            jax.ShapeDtypeStruct((DC, NY * FS), F32),
            jax.ShapeDtypeStruct((1, DX), F32),
        ),
        in_specs=[spec] * 5,
        out_specs=(spec,) * 5,
    )(*parts)
    return out.T, d_tokens.T, grad_up, grad_down.T, grad_gain.reshape(DX)


def solution(mesh):
    in_specs = (
        P(("depth", "col"), "row"),
        P("row"),
        P("col", "row"),
        P("row", "col"),
        P(("depth", "col"), "row"),
    )
    out_specs = (
        P(("depth", "col"), "row"),
        P(("depth", "col"), "row"),
        P("col", "row"),
        P("row", "col"),
        P("row"),
    )
    return jax.shard_map(
        on_device, mesh=mesh, in_specs=in_specs, out_specs=out_specs, check_vma=False
    )
```

```python
import math

import jax
import jax.numpy as jnp
from jax import lax
from jax.experimental import pallas as pl
from jax.experimental.pallas import tpu as pltpu
from jax.sharding import PartitionSpec as P

EPS = 1e-06
MESH = pl.DeviceIdType.MESH
F32, BF16 = jnp.float32, jnp.bfloat16

NX, NY, NZ = 4, 4, 8
D, FF, TOK = 3200, 6400, 8192
DX = D // NX
TB = 128
T = NY * TB
DZ = D // NZ
DC = D // (NY * NZ)
FS = FF // (NX * NY)
FP = 512
RP = 112
EX = 16
DE = DX + EX
FM = 384
HALF = ((0, 400), (400, 400))
HALFE = ((0, 400), (400, 416))
ORDER = (2, 1, -1, 0)
ZORDER = (4, 3, -3, 2, -2, 1, -1, 0)
SCALE = TOK ** (-0.5)


def gelu_value(pre):
    return 0.5 * pre * (1.0 + lax.erf(pre / math.sqrt(2.0)))


def gelu_slope(pre):
    return 0.5 * (1.0 + lax.erf(pre / math.sqrt(2.0))) + pre * jnp.exp(
        -0.5 * pre * pre
    ) / math.sqrt(2.0 * math.pi)


def dot(left, right, left_dim, right_dim):
    return lax.dot_general(
        left, right, (((left_dim,), (right_dim,)), ((), ())), preferred_element_type=F32
    )


class Messages:
    def __init__(self, send, recv):
        self.send, self.recv, self.n, self.live = send, recv, 0, []

    def start(self, src, dst, device):
        i = self.n
        self.n += 1
        cp = pltpu.make_async_remote_copy(
            src_ref=src, dst_ref=dst, send_sem=self.send.at[i], recv_sem=self.recv.at[i],
            device_id=device, device_id_type=MESH,
        )
        cp.start()
        self.live.append(cp)
        return cp

    def drain(self):
        for cp in self.live:
            cp.wait_send()
        self.live = []


N_MESSAGES = 224

GATHER = (
    ("wa",), ("xm",), ("cm",), ("wz", 3), ("xn", 0), ("cn", 0), ("gs",), ("wr",), ("wz", 1), ("wf", 0, 0, 3),
    ("wf", 0, 1, 3), ("wz", 2), ("xf", 0), ("xf", 1), ("xn", 1), ("xn", -1), ("wf", 0, 0, 1), ("wf", 0, 1, 1),
    ("cf", 0), ("cf", 1), ("cn", 1), ("wf", 1, 1, 3), ("cn", -1), ("wf", 1, 0, 3), ("cg", 0, 0), ("cg", 0, 1),
    ("wf", 0, 0, 2), ("wf", 0, 1, 2), ("wf", 1, 0, 1), ("wf", 1, 1, 1), ("xn", 2), ("nm", 0), ("xg", 0, 0),
    ("xg", 0, 1), ("wz", 0), ("wu", 0), ("wf", 2, 1, 3), ("wf", 1, 0, 2), ("wf", 1, 1, 2), ("cg", 1, 0), ("cg", 1, 1),
    ("wf", 2, 1, 1), ("xg", 1, 0), ("xg", 1, 1), ("wf", 0, 0, 0), ("wf", 0, 1, 0), ("wu", -1), ("wu", 1),
    ("cg", -1, 0), ("cg", -1, 1), ("wf", 2, 0, 2), ("xg", -1, 0), ("xg", -1, 1), ("wf", 1, 0, 0), ("wu", -2),
    ("cn", 2), ("wf", 1, 1, 0), ("wf", 2, 0, 0), ("wu", 2), ("wu", -3), ("xg", 2, 0), ("xg", 2, 1), ("nm", -1),
    ("nm", 1), ("wu", 3), ("wu", 4), ("cg", 2, 0), ("cg", 2, 1), ("ww",), ("db", 0), ("db", -1), ("db", 1), ("db", 2),
    ("nm", 2), ("pc",), ("gl",), ("hp",),
)

SCHEDULE = (
    ("B", 2), ("N", 2), ("G", 0), ("b0", 2), ("N", 1), ("B", 1), ("b0", 1), ("B", -1), ("N", -1), ("b0", -1),
    ("d0", 2), ("G", 1), ("F", 0), ("Z", 0, 0, 0), ("Z", 0, 1, 1), ("Z", 0, 0, 2), ("G", 2), ("b1", 2, 0),
    ("b1", 2, 1), ("B", 0), ("G", 3), ("G", 4), ("b1", 1, 1), ("d1", 2, 0), ("d1", 2, 1), ("Z", 0, 1, 3), ("F", 1),
    ("F", 2), ("Z", 1, 1, 0), ("Z", 1, 0, 0), ("Z", 1, 1, 1), ("Z", 1, 0, 1), ("G", 7), ("b1", -1, 1), ("b1", -1, 0),
    ("G", 5), ("Z", 1, 0, 2), ("b1", 1, 0), ("Z", 1, 1, 2), ("d0", -1), ("F", 3), ("b0", 0), ("N", 0), ("G", 6),
    ("Z", 2, 0, 0), ("F", 4), ("Z", 1, 1, 3), ("d0", 1), ("Z", 1, 0, 3), ("F", 7), ("Z", 2, 1, 0), ("P", 3), ("F", 5),
    ("Z", 2, 0, 1), ("P", 1), ("P", 7), ("P", 5), ("F", 6), ("Z", 2, 1, 1), ("P", 0), ("d1", -1, 0), ("d1", -1, 1),
    ("Z", 2, 0, 2), ("P", 2), ("P", 6), ("Z", 2, 1, 2), ("P", 4), ("g", 0), ("d2",), ("Z", 3, 0, 0), ("d0", 0),
    ("b2",), ("d1", 1, 1), ("d1", 1, 0), ("Z", 2, 1, 3), ("Z", 2, 0, 3), ("Z", 3, 1, 0), ("Z", 3, 0, 1),
    ("Z", 3, 1, 1), ("g", 1), ("Z", 3, 0, 2), ("Z", 3, 1, 2), ("b1", 0, 0), ("b1", 0, 1), ("d1", 0, 1), ("d1", 0, 0),
    ("Z", 3, 1, 3), ("Z", 3, 0, 3), ("d3", 1), ("g", 2), ("b3", 1), ("b3", 0), ("ZF", 0), ("ZF", 1), ("ZF", 2),
    ("d3", 0), ("g", 3), ("ZF", 3), ("g", 4), ("H", 0), ("g", 5), ("H", 1), ("H", 2), ("AO",), ("g", 6), ("AE",),
    ("RB",), ("RD",),
)


def kernel(
    x_in, c_in, up_in, down_in, g_in,
    out_hbm, dtok_hbm, gu_hbm, gd_hbm, gg_ref,
    xo, co, ws, w_in, wz, out_ref, dtok_ref, go, xt, nc, w, relay, gr, gcol, inv_s, pre_s, dh_s, slope, hd, md_s, gs, g, xr, zs, zr,
    br, dn, b0, b1, bq0, bq1, d0, d1, dq0, dq1, stage, ga, ggp, ggr, ggx, ggy, ggz, ggc,
    send_sem, recv_sem, copy_sem,
):
    x = lax.axis_index("row")
    col = lax.axis_index("col")
    d = lax.axis_index("depth")
    y, z = lax.rem(col, NY), col // NY
    e = 1 - d

    def dev(ax=None, off=0):
        xx, yy, zz, dd = x, y, z, d
        if ax == "x":
            xx = lax.rem(x + (off + NX), NX)
        elif ax == "y":
            yy = lax.rem(y + (off + NY), NY)
        elif ax == "z":
            zz = lax.rem(z + (off + NZ), NZ)
        elif ax == "c":
            dd = e
        return (xx, zz * NY + yy, dd)

    def px(off):
        return lax.rem(x + (off + NX), NX)

    def py(off):
        return lax.rem(y + (off + NY), NY)

    def pz(off):
        return lax.rem(z + (off + NZ), NZ)

    def rows(i, size, off=0, n=None):
        return pl.ds(pl.multiple_of(i * size + off, 16), size if n is None else n)

    def lanes(i):
        return pl.ds(pl.multiple_of(i * TB, TB), TB)

    msg = Messages(send_sem, recv_sem)

    barrier = pltpu.get_barrier_semaphore()
    partners = [("x", 1), ("x", -1), ("x", 2), ("y", 1), ("y", -1), ("y", 2), ("z", 1), ("z", -1), ("c", 0)]
    for ax, off in partners:
        pl.semaphore_signal(barrier, inc=1, device_id=dev(ax, off), device_id_type=MESH)

    loads = [pltpu.make_async_copy(x_in, xo, copy_sem.at[0]), pltpu.make_async_copy(c_in, co, copy_sem.at[1])]
    for cp in loads:
        cp.start()

    @pl.when(d == 0)
    def _():
        cp = pltpu.make_async_copy(up_in, ws, copy_sem.at[2])
        cp.start()
        cp.wait()

    @pl.when(d == 1)
    def _():
        cp = pltpu.make_async_copy(down_in, ws, copy_sem.at[2])
        cp.start()
        cp.wait()

    w_in[...] = jnp.zeros_like(w_in)
    for j in range(NY):
        w_in[j, pl.ds(0, DC)] = ws[:, j * FS:j * FS + FM]
        tail = jnp.concatenate([ws[:, j * FS + FM:(j + 1) * FS].astype(F32), jnp.zeros((DC, TB - 16), F32)], axis=1)
        tail = jnp.concatenate([tail, jnp.zeros((TB - DC, TB), F32)], axis=0).T
        w_in[j, pl.ds(RP - 16, 16), pl.ds(0, 2 * TB)] = jnp.concatenate([
            jnp.concatenate([ws[RP - 16:DC, j * FS:j * FS + 2 * TB].astype(F32),
                             jnp.zeros((RP - 8 - DC, 2 * TB), F32)], axis=0),
            jnp.concatenate([tail[:8], tail[8:16]], axis=1)], axis=0).astype(BF16)
    for cp in loads:
        cp.wait()
    xt[rows(x, DX), lanes(y)] = xo[...]
    nc[1, rows(x, DX), lanes(y)] = co[...]
    gain_own = g_in[...].astype(F32).reshape(1, DX)
    gr[x] = jnp.zeros_like(gr[0])
    gr[x, :, pl.ds(0, DX)] = jnp.broadcast_to(gain_own, (8, DX))
    pl.semaphore_wait(barrier, len(partners))

    class Gather:
        def __init__(self, ref, first, second):
            self.ref, self.a, self.b = ref, first, second
            self.n1, self.n2, self.m2 = {}, {}, {}

        def at(self, a, b, half=None):
            xi, yi = (px(a), py(b)) if self.a == "x" else (px(b), py(a))
            off, n = (0, DX) if half is None else HALF[half]
            return self.ref(rows(xi, DX, off, n), lanes(yi))

        def go(self, a, b, ax, off, half=None):
            ref = self.at(a, b, half)
            return msg.start(ref, ref, dev(ax, off))

        def first(self):
            self.m1 = [self.go(0, 0, self.a, 1), self.go(0, 0, self.a, -1)]

        def second(self, a):
            self.n1[a] = [self.go(a, 0, self.b, 1), self.go(a, 0, self.b, -1)]

        def first_forward(self, s):
            self.m1[s].wait_recv()
            self.m2[s] = self.go(2 * s - 1, 0, self.a, 1 - 2 * s, s)

        def first_done(self):
            while self.m2:
                self.m2.popitem()[1].wait_recv()

        def second_step(self, a):
            if a == 2:
                self.first_done()
            self.second(a)

        def second_forward(self, a, s):
            self.n1[a][s].wait_recv()
            self.n2[a, s] = self.go(a, 2 * s - 1, self.b, 1 - 2 * s, s)

        def second_done(self):
            for a in ORDER:
                for s in (0, 1):
                    self.n2[a, s].wait_recv()

    gx = Gather(lambda r, l: xt.at[r, l], "x", "y")
    gc = Gather(lambda r, l: nc.at[1, r, l], "y", "x")

    gain_msgs = [msg.start(gr.at[x], gr.at[x], dev("x", off)) for off in (1, -1, 2)]

    def pack_parts(k, val):
        tail = jnp.concatenate([val[:, FM:], jnp.zeros((FP - DZ, FP - FM), F32)], axis=0).T[:16]
        for q in range(NY):
            g[k, q, pl.ds(0, DC)] = val[q * DC:(q + 1) * DC, :FM]
            for i in (0, 1):
                g[k, q, pl.ds(RP - 8, 8), pl.ds(i * TB, TB)] = tail[i * 8:i * 8 + 8, q * DC:q * DC + TB]

    def unpack_part(val):
        tail = jnp.concatenate([val[RP - 8:, :TB], val[RP - 8:, TB:2 * TB], jnp.zeros((TB - 16, TB), F32)], axis=0)
        return jnp.concatenate([val[:DC], tail.T[:DC]], axis=1)

    a2a, zw, wc = {}, {}, {}
    late = {0: (0, 2), 1: (1, 3)}

    def w_at(off, j):
        return wz.at[pz(off), py(ORDER[j])]

    def w_apart():
        a2a[0] = msg.start(w_in.at[py(2)], relay, dev("y", 1 - 2 * d))
        for i in (1, 2):
            a2a[i] = msg.start(w_in.at[py(ORDER[i])], wz.at[z, y], dev("y", ORDER[i]))
        wz[z, y] = w_in[y]

    def w_relay():
        a2a[0].wait_recv()
        a2a[0] = msg.start(relay, wz.at[z, py(2 * d - 1)], dev("y", 1 - 2 * d))

    def w_first(j):
        if j < 3:
            a2a[(0, 2, 1)[j]].wait_recv()
        for p in (0, 1):
            zw[0, p, j] = msg.start(w_at(0, j), w_at(0, j), dev("z", 1 - 2 * p))

    def w_forward(s, p, j):
        zw[s, p, j].wait_recv()
        ref = w_at((2 * p - 1) * (s + 1), j)
        zw[s + 1, p, j] = msg.start(ref, ref, dev("z", 1 - 2 * p))

    def w_unpack(off):
        s = abs(off) - 1
        for p in (0, 1):
            for j in range(NY):
                if (s == 3 and j in late[p]) or (s == 2 and off == (2 * p - 1) * 3 and j not in late[p]):
                    zw[s, p, j].wait_recv()
        zc = pz(off)
        r = rows(zc, DZ)
        w[d, r] = jnp.concatenate([unpack_part(wz[zc, q].astype(F32)) for q in range(NY)], axis=0).astype(BF16)
        wc[off] = msg.start(w.at[d, r], w.at[d, r], dev("c"))

    def w_done():
        for cp in wc.values():
            cp.wait_recv()

    def spread_gain(i, carry):
        column = gr[i].T[:DX, 0:1]
        gcol[i] = jnp.broadcast_to(column, (DX, TB))
        return carry

    def all_gain():
        for cp in gain_msgs:
            cp.wait_recv()
        lax.fori_loop(0, NX, spread_gain, 0)

    def normalise(off):
        yi = py(off)
        if off == 0:
            gx.first_done()
        if off == 2:
            gx.second_done()

        def square(i, acc):
            v = xt[pl.ds(pl.multiple_of(i * 160, 16), 160), lanes(yi)].astype(F32)
            return acc + jnp.sum(v * v, axis=0, keepdims=True)

        total = lax.fori_loop(0, D // 160, square, jnp.zeros((1, TB), F32))
        inv = lax.rsqrt(total / D + EPS)
        if off == 0:
            inv_s[...] = inv

        def scale(i, carry):
            xi, k = i // 5, lax.rem(i, 5)
            r = pl.ds(pl.multiple_of(i * 160, 16), 160)
            v = xt[r, lanes(yi)].astype(F32) * inv
            nc[0, r, lanes(yi)] = (v * gcol[xi, pl.ds(pl.multiple_of(k * 160, 16), 160)]).astype(BF16)
            return carry

        lax.fori_loop(0, D // 160, scale, 0)

    def pre_all():
        pre_s[...] = jnp.zeros_like(pre_s)

        def body(i, carry):
            r = rows(i, 2 * DZ)
            pre_s[...] += dot(w[0, r], nc[0, r], 0, 0)
            return carry

        lax.fori_loop(0, NZ // 2, body, 0)

    def activate():
        def body(i, carry):
            r = pl.ds(pl.multiple_of(i * 16, 16), 16)
            pre = pre_s[r]
            hd[1, r] = gelu_value(pre).astype(BF16)
            slope[r] = gelu_slope(pre)
            return carry

        lax.fori_loop(0, FS // 16, body, 0)

    def d_hidden_rows(a):
        if a == 0:
            gc.first_done()
            dh_s[...] = jnp.zeros_like(dh_s)
        if a == 2:
            gc.second_done()
        r = rows(px(a), DX)
        dh_s[...] += dot(w[1, r], nc[1, r], 0, 0)

    def d_pre():
        def body(i, acc):
            r = pl.ds(pl.multiple_of(i * 16, 16), 16)
            dpre = dh_s[r] * slope[r]
            hd[0, r] = dpre.astype(BF16)
            return acc + jnp.sum(dpre * pre_s[r], axis=0, keepdims=True)

        md_s[...] = lax.fori_loop(0, FS // 16, body, jnp.zeros((1, T), F32))

    hd[0, pl.ds(FS, FP - FS)] = jnp.zeros((FP - FS, T), BF16)
    hd[1, pl.ds(FS, FP - FS)] = jnp.zeros((FP - FS, T), BF16)
    steps = {
        "xm": gx.first, "xf": gx.first_forward, "xn": gx.second_step, "xg": gx.second_forward,
        "cm": gc.first, "cf": gc.first_forward, "cn": gc.second_step, "cg": gc.second_forward,
        "wa": w_apart, "wr": w_relay, "wz": w_first, "wf": w_forward, "wu": w_unpack, "ww": w_done,
        "gs": all_gain, "nm": normalise, "pc": pre_all, "gl": activate, "db": d_hidden_rows,
        "hp": d_pre,
    }
    for name, *where in GATHER:
        steps[name](*where)
    msg.drain()

    core = {}
    ggr[...] = jnp.zeros_like(ggr)
    g[...] = jnp.zeros_like(g)
    ones = jnp.ones((8, FP), BF16)

    def fold(k):
        core[k].wait_recv()
        total = gs[k] + xr[k].astype(F32)
        pack_parts(k, total)
        gs[k] = total

    def gain_part(k):
        zc = pz(ZORDER[k])
        v = gs[k] * w[d, rows(zc, DZ)].astype(F32)
        high = v.astype(BF16)
        low = (v - high.astype(F32)).astype(BF16)
        ggr[:, pl.ds(0, DZ)] = dot(ones, high, 1, 1) + dot(ones, low, 1, 1)
        for j in range(4):
            ggp[zc // 2, pl.ds(lax.rem(zc, 2) * 4 + j, 1), :] = ggr[0:1, j * TB:(j + 1) * TB]

    def gain_x():
        return [msg.start(ggp.at[px(off)], ggx.at[i], dev("x", off)) for i, off in enumerate((1, -1, 2))]

    def gain_y(cps):
        for cp in cps:
            cp.wait_recv()
        ggy[0] = ggp[x] + ggx[0] + ggx[1] + ggx[2]
        return [msg.start(ggy.at[0], ggy.at[1 + i], dev("y", off)) for i, off in enumerate((1, -1, 2))]

    def gain_z(cps):
        for cp in cps:
            cp.wait_recv()
        ggz[0] = ggy[0] + ggy[1] + ggy[2] + ggy[3]
        return [msg.start(ggz.at[0], ggz.at[1 + p], dev("z", 1 - 2 * p)) for p in (0, 1)]

    def gain_ring(cps, s):
        for cp in cps:
            cp.wait_recv()
        return [
            msg.start(ggz.at[2 * s - 1 + p], ggz.at[2 * s + 1 + p], dev("z", 1 - 2 * p))
            for p in ((0, 1) if s < 3 else (0,))
        ]

    def gain_c(cps):
        for cp in cps:
            cp.wait_recv()
        total = ggz[0]
        for i in range(NZ - 1):
            total = total + ggz[1 + i]
        ggc[0] = total
        return [msg.start(ggc.at[0], ggc.at[1], dev("c"))]

    def grad_chunk(k):
        r = rows(pz(ZORDER[k]), DZ)
        xt[pl.ds(k * DZ, DZ)] = dot(nc[e, r], hd[e], 1, 1).astype(BF16)
        core[k] = msg.start(xt.at[pl.ds(k * DZ, DZ)], xr.at[k], dev("c"))
        gs[k] = dot(nc[d, r], hd[d], 1, 1)

    zmsg = {}

    def z_reduce(s, p, j):
        k = 0 if s == 0 else 2 * s - 1 + p
        q = py(ORDER[j])
        val = g[k, q]
        if (s - 1, p, j) in zmsg:
            zmsg[s - 1, p, j].wait_recv()
            val = val + zr[p, s - 1, q].astype(F32)
        zs[p, s, q] = val.astype(BF16)
        zmsg[s, p, j] = msg.start(zs.at[p, s, q], zr.at[p, s, q], dev("z", 1 - 2 * p))

    back, hands = {}, {}

    def z_final(j):
        q = py(ORDER[j])
        for p in (0, 1):
            zmsg[3, p, j].wait_recv()
        val = (g[7, q] + zr[0, 3, q].astype(F32) + zr[1, 3, q].astype(F32)).astype(BF16)
        if j < 3:
            stage[j] = val
            back[j] = msg.start(stage.at[j], ga.at[d, y], dev("y", ORDER[j]))
        else:
            ga[d, y] = val
            hands[j] = msg.start(ga.at[d, y], ga.at[d, y], dev("c"))

    def hand_on(j):
        back[j].wait_recv()
        ref = ga.at[d, py(-ORDER[j])]
        hands[j] = msg.start(ref, ref, dev("c"))

    def assemble(i):
        for j in range(NY):
            go[i, :, pl.ds(j * FS, FS)] = unpack_part(ga[i, j].astype(F32))[:, :FS].astype(BF16)

    class Reduce:
        def __init__(self, ref, a, b, halves, r0, r1, q0, q1):
            self.ref, self.a, self.b, self.h = ref, a, b, halves
            self.r0, self.r1, self.q0, self.q1 = r0, r1, q0, q1
            self.p0, self.p1, self.m1 = {}, {}, {}

        def at(self, a, b):
            return (px(a), py(b)) if self.a == "x" else (px(b), py(a))

        def send0(self, b):
            i = ORDER.index(b)
            xi, yi = self.at(2, b)
            self.p0[b] = []
            for s in (0, 1):
                o, n = self.h[s]
                self.p0[b].append(msg.start(
                    self.ref.at[xi, yi, pl.ds(o, n)], self.r0.at[i, s, pl.ds(0, n)], dev(self.a, 1 - 2 * s)))

        def send1(self, b, s):
            i = ORDER.index(b)
            o, n = self.h[s]
            xi, yi = self.at(1 - 2 * s, b)
            self.p0[b][s].wait_recv()
            self.ref[xi, yi, pl.ds(o, n)] = (
                self.ref[xi, yi, pl.ds(o, n)].astype(F32) + self.r0[i, s, pl.ds(0, n)].astype(F32)
            ).astype(BF16)
            self.p1[b, s] = msg.start(self.ref.at[xi, yi], self.r1.at[i, s], dev(self.a, 1 - 2 * s))

        def sum1(self, b):
            i = ORDER.index(b)
            xi, yi = self.at(0, b)
            for s in (0, 1):
                self.p1[b, s].wait_recv()
            return self.ref[xi, yi].astype(F32) + self.r1[i, 0].astype(F32) + self.r1[i, 1].astype(F32)

        def second0(self):
            xi, yi = self.at(0, 2)
            self.ref[xi, yi] = self.sum1(2).astype(BF16)
            self.m0 = []
            for s in (0, 1):
                o, n = self.h[s]
                self.m0.append(msg.start(
                    self.ref.at[xi, yi, pl.ds(o, n)], self.q0.at[s, pl.ds(0, n)], dev(self.b, 1 - 2 * s)))

        def second1(self, s):
            b = 1 - 2 * s
            xi, yi = self.at(0, b)
            o, n = self.h[s]
            total = self.sum1(b)
            self.m0[s].wait_recv()
            self.ref[xi, yi, pl.ds(o, n)] = (
                total[o:o + n] + self.q0[s, pl.ds(0, n)].astype(F32)).astype(BF16)
            so, sn = self.h[1 - s]
            self.ref[xi, yi, pl.ds(so, sn)] = total[so:so + sn].astype(BF16)
            self.m1[s] = msg.start(self.ref.at[xi, yi], self.q1.at[s], dev(self.b, b))

        def result(self):
            total = self.sum1(0)
            for s in (0, 1):
                self.m1[s].wait_recv()
            return total + self.q1[0].astype(F32) + self.q1[1].astype(F32)

    rb = Reduce(br, "y", "x", HALF, b0, b1, bq0, bq1)
    rd = Reduce(dn, "x", "y", HALFE, d0, d1, dq0, dq1)

    def branch_block(off):
        xi = px(off)
        val = dot(w[1, rows(xi, DX)], hd[1], 1, 0).astype(BF16)
        for j in range(NY):
            br[xi, j] = val[:, j * TB:(j + 1) * TB]

    def normed_block(off):
        xi = px(off)
        val = dot(w[0, rows(xi, DX)], hd[0], 1, 0).astype(BF16)
        for j in range(NY):
            dn[xi, j, pl.ds(0, DX)] = val[:, j * TB:(j + 1) * TB]
            dn[xi, j, pl.ds(DX, EX)] = jnp.broadcast_to(
                md_s[:, j * TB:(j + 1) * TB], (EX, TB)).astype(BF16)

    def out_result():
        out_ref[...] = (xo[...].astype(F32) + rb.result()).astype(BF16)
        stores[0].start()

    def dtok_result():
        total = rd.result()
        dnorm = total[:DX]
        inv = inv_s[...]
        mean_dot = total[DX:DX + 1] / D
        unit = xo[...].astype(F32) * inv
        dtok_ref[...] = (
            co[...].astype(F32) + inv * (dnorm * gcol[x] - unit * mean_dot)
        ).astype(BF16)
        stores[1].start()

    chain = [gain_x, gain_y, gain_z, lambda m: gain_ring(m, 1), lambda m: gain_ring(m, 2),
             lambda m: gain_ring(m, 3), gain_c]
    gain = None

    def gain_step(i):
        nonlocal gain
        gain = chain[i](gain) if i else chain[0]()

    stores = [
        pltpu.make_async_copy(src, dst, copy_sem.at[i])
        for i, (src, dst) in enumerate((
            (out_ref, out_hbm), (dtok_ref, dtok_hbm), (go.at[0], gu_hbm), (go.at[1], gd_hbm)))
    ]

    def other_core():
        for j in range(NY):
            hands[j].wait_recv()
        assemble(e)

    steps = {
        "B": branch_block, "N": normed_block, "G": grad_chunk, "F": fold, "P": gain_part,
        "Z": z_reduce, "ZF": z_final, "H": hand_on, "AO": lambda: assemble(d), "AE": other_core,
        "b0": rb.send0, "b1": rb.send1, "b2": rb.second0, "b3": rb.second1, "RB": out_result,
        "d0": rd.send0, "d1": rd.send1, "d2": rd.second0, "d3": rd.second1, "RD": dtok_result,
        "g": gain_step,
    }
    for name, *where in SCHEDULE:
        steps[name](*where)

    for i in (2, 3):
        stores[i].start()
    for cp in gain:
        cp.wait_recv()
    total = jnp.where(d == 0, ggc[0], ggc[1]) * SCALE
    for i in (0, 1):
        row = jnp.concatenate([total[4 * i + j:4 * i + j + 1] for j in range(4)], axis=1)
        gg_ref[:, pl.ds(i * DZ, DZ)] = row[:, :DZ]
    gg_ref[...] = gg_ref[...] / gain_own
    assert msg.n <= N_MESSAGES
    msg.drain()
    for cp in stores:
        cp.wait()


def vm(shape, dtype=BF16):
    return pltpu.VMEM(shape, dtype)


def block(x, c, up, down, g):
    spec = pl.BlockSpec(memory_space=pltpu.VMEM)
    anywhere = pl.BlockSpec(memory_space=pl.ANY)
    return pl.pallas_call(
        kernel,
        out_shape=(
            jax.ShapeDtypeStruct((DX, TB), BF16),
            jax.ShapeDtypeStruct((DX, TB), BF16),
            jax.ShapeDtypeStruct((DC, NY * FS), BF16),
            jax.ShapeDtypeStruct((DC, NY * FS), BF16),
            jax.ShapeDtypeStruct((1, DX), F32),
        ),
        in_specs=[anywhere] * 4 + [spec],
        out_specs=(anywhere,) * 4 + (spec,),
        scratch_shapes=[
            vm((DX, TB)),
            vm((DX, TB)),
            vm((DC, NY * FS)),
            vm((NY, RP, FM)),
            vm((NZ, NY, RP, FM)),
            vm((DX, TB)),
            vm((DX, TB)),
            vm((2, DC, NY * FS)),
            vm((D, T)),
            vm((2, D, T)),
            vm((2, D, FP)),
            vm((RP, FM)),
            vm((NX, 8, 896), F32),
            vm((NX, DX, TB), F32),
            vm((1, TB), F32),
            vm((FP, T), F32),
            vm((FP, T), F32),
            vm((FS, T), F32),
            vm((2, FP, T)),
            vm((1, T), F32),
            vm((NZ, DZ, FP), F32),
            vm((NZ, NY, RP, FM), F32),
            vm((NZ, DZ, FP)),
            vm((2, 4, NY, RP, FM)),
            vm((2, 4, NY, RP, FM)),
            vm((NX, NY, DX, TB)),
            vm((NX, NY, DE, TB)),
            vm((4, 2, 400, TB)),
            vm((4, 2, DX, TB)),
            vm((2, 400, TB)),
            vm((2, DX, TB)),
            vm((4, 2, 416, TB)),
            vm((4, 2, DE, TB)),
            vm((2, 416, TB)),
            vm((2, DE, TB)),
            vm((3, RP, FM)),
            vm((2, NY, RP, FM)),
            vm((NX, 8, TB), F32),
            vm((8, FP), F32),
            vm((3, 8, TB), F32),
            vm((4, 8, TB), F32),
            vm((NZ, 8, TB), F32),
            vm((2, 8, TB), F32),
            pltpu.SemaphoreType.DMA((N_MESSAGES,)),
            pltpu.SemaphoreType.DMA((N_MESSAGES,)),
            pltpu.SemaphoreType.DMA((4,)),
        ],
        compiler_params=pltpu.CompilerParams(
            collective_id=0, has_side_effects=True, vmem_limit_bytes=60 * 2**20
        ),
    )(x, c, up, down, g)


def finish(out_in, dtok_in, gu_in, gd_in, gg_in, out_ref, dtok_ref, gu_ref, gd_ref, gg_ref):
    out_ref[...] = out_in[...]
    dtok_ref[...] = dtok_in[...]
    gu_ref[...] = gu_in[...].astype(F32) * SCALE
    gd_ref[...] = gd_in[...].astype(F32) * SCALE
    gg_ref[...] = gg_in[...].reshape(DX)


def on_device(tokens, gain, w_up, w_down, cotangent):
    parts = block(tokens.T, cotangent.T, w_up, w_down.T, gain)
    spec = pl.BlockSpec(memory_space=pltpu.VMEM)
    out, d_tokens, grad_up, grad_down, grad_gain = pl.pallas_call(
        finish,
        out_shape=(
            jax.ShapeDtypeStruct((DX, TB), BF16),
            jax.ShapeDtypeStruct((DX, TB), BF16),
            jax.ShapeDtypeStruct((DC, NY * FS), F32),
            jax.ShapeDtypeStruct((DC, NY * FS), F32),
            jax.ShapeDtypeStruct((DX,), F32),
        ),
        in_specs=[spec] * 5,
        out_specs=(spec,) * 5,
    )(*parts)
    return out.T, d_tokens.T, grad_up, grad_down.T, grad_gain


def solution(mesh):
    in_specs = (
        P(("depth", "col"), "row"),
        P("row"),
        P("col", "row"),
        P("row", "col"),
        P(("depth", "col"), "row"),
    )
    out_specs = (
        P(("depth", "col"), "row"),
        P(("depth", "col"), "row"),
        P("col", "row"),
        P("row", "col"),
        P("row"),
    )
    return jax.shard_map(
        on_device, mesh=mesh, in_specs=in_specs, out_specs=out_specs, check_vma=False
    )
```

```python
import math

import jax
import jax.numpy as jnp
from jax import lax
from jax.experimental import pallas as pl
from jax.experimental.pallas import tpu as pltpu
from jax.sharding import PartitionSpec as P

EPS = 1e-06
MESH = pl.DeviceIdType.MESH
F32, BF16 = jnp.float32, jnp.bfloat16

NX, NY, NZ = 4, 4, 8
D, FF, TOK = 3200, 6400, 8192
DX = D // NX
TB = 128
T = NY * TB
DZ = D // NZ
DC = D // (NY * NZ)
FS = FF // (NX * NY)
FP = 512
RP = 112
EX = 16
DE = DX + EX
FM = 384
HALF = ((0, 400), (400, 400))
HALFE = ((0, 400), (400, 416))
ORDER = (2, 1, -1, 0)
ZORDER = (4, 3, -3, 2, -2, 1, -1, 0)
SCALE = TOK ** (-0.5)


def gelu_value(pre):
    return 0.5 * pre * (1.0 + lax.erf(pre / math.sqrt(2.0)))


def gelu_slope(pre):
    return 0.5 * (1.0 + lax.erf(pre / math.sqrt(2.0))) + pre * jnp.exp(
        -0.5 * pre * pre
    ) / math.sqrt(2.0 * math.pi)


def dot(left, right, left_dim, right_dim):
    return lax.dot_general(
        left, right, (((left_dim,), (right_dim,)), ((), ())), preferred_element_type=F32
    )


class Message:
    def __init__(self, copy, pool, i):
        self.copy, self.pool, self.i = copy, pool, i

    def wait_recv(self):
        self.copy.wait_recv()
        self.copy.wait_send()
        self.pool.append(self.i)


class Messages:
    def __init__(self, send, recv):
        self.send, self.recv, self.n, self.n_send, self.pool = send, recv, 0, 0, []

    def start(self, src, dst, device):
        if self.pool:
            i = self.pool.pop(0)
        else:
            i = self.n_send
            self.n_send += 1
        cp = pltpu.make_async_remote_copy(
            src_ref=src, dst_ref=dst, send_sem=self.send.at[i], recv_sem=self.recv.at[self.n],
            device_id=device, device_id_type=MESH,
        )
        self.n += 1
        cp.start()
        return Message(cp, self.pool, i)


N_MESSAGES, N_SEND = 180, 29

GATHER = (
    ("wa",), ("xm",), ("cm",), ("wz", 3), ("xn", 0), ("cn", 0), ("gs",), ("wr",), ("wz", 1), ("wf", 0, 0, 3),
    ("wf", 0, 1, 3), ("wz", 2), ("xf", 0), ("xf", 1), ("xn", 1), ("xn", -1), ("wf", 0, 0, 1), ("wf", 0, 1, 1),
    ("cf", 0), ("cf", 1), ("cn", 1), ("wf", 1, 1, 3), ("cn", -1), ("wf", 1, 0, 3), ("cg", 0, 0), ("cg", 0, 1),
    ("wf", 0, 0, 2), ("wf", 0, 1, 2), ("wf", 1, 0, 1), ("wf", 1, 1, 1), ("xn", 2), ("nm", 0), ("xg", 0, 0),
    ("xg", 0, 1), ("wz", 0), ("wu", 0), ("wf", 2, 1, 3), ("wf", 1, 0, 2), ("wf", 1, 1, 2), ("cg", 1, 0), ("cg", 1, 1),
    ("wf", 2, 1, 1), ("xg", 1, 0), ("xg", 1, 1), ("wf", 0, 0, 0), ("wf", 0, 1, 0), ("wu", -1), ("wu", 1),
    ("cg", -1, 0), ("cg", -1, 1), ("wf", 2, 0, 2), ("xg", -1, 0), ("xg", -1, 1), ("wf", 1, 0, 0), ("wu", -2),
    ("cn", 2), ("wf", 1, 1, 0), ("wf", 2, 0, 0), ("wu", 2), ("wu", -3), ("xg", 2, 0), ("xg", 2, 1), ("nm", -1),
    ("nm", 1), ("wu", 3), ("wu", 4), ("cg", 2, 0), ("cg", 2, 1), ("ww",), ("db", 0), ("db", -1), ("db", 1), ("db", 2),
    ("nm", 2), ("pc",), ("gl",), ("hp",),
)

SCHEDULE = (
    ("B", 2), ("N", 2), ("G", 0), ("b0", 2), ("N", 1), ("B", 1), ("b0", 1), ("B", -1), ("N", -1), ("b0", -1),
    ("d0", 2), ("G", 1), ("F", 0), ("Z", 0, 0, 0), ("Z", 0, 1, 1), ("Z", 0, 0, 2), ("G", 2), ("b1", 2, 0),
    ("b1", 2, 1), ("B", 0), ("G", 3), ("G", 4), ("b1", 1, 1), ("d1", 2, 0), ("d1", 2, 1), ("Z", 0, 1, 3), ("F", 1),
    ("F", 2), ("Z", 1, 1, 0), ("Z", 1, 0, 0), ("Z", 1, 1, 1), ("Z", 1, 0, 1), ("G", 7), ("b1", -1, 1), ("b1", -1, 0),
    ("G", 5), ("Z", 1, 0, 2), ("b1", 1, 0), ("Z", 1, 1, 2), ("d0", -1), ("F", 3), ("b0", 0), ("N", 0), ("G", 6),
    ("Z", 2, 0, 0), ("F", 4), ("Z", 1, 1, 3), ("d0", 1), ("Z", 1, 0, 3), ("F", 7), ("Z", 2, 1, 0), ("P", 3), ("F", 5),
    ("Z", 2, 0, 1), ("P", 1), ("P", 7), ("P", 5), ("F", 6), ("Z", 2, 1, 1), ("P", 0), ("d1", -1, 0), ("d1", -1, 1),
    ("Z", 2, 0, 2), ("P", 2), ("P", 6), ("Z", 2, 1, 2), ("P", 4), ("g", 0), ("d2",), ("Z", 3, 0, 0), ("d0", 0),
    ("b2",), ("d1", 1, 1), ("d1", 1, 0), ("Z", 2, 1, 3), ("Z", 2, 0, 3), ("Z", 3, 1, 0), ("Z", 3, 0, 1),
    ("Z", 3, 1, 1), ("g", 1), ("Z", 3, 0, 2), ("Z", 3, 1, 2), ("b1", 0, 0), ("b1", 0, 1), ("d1", 0, 1), ("d1", 0, 0),
    ("Z", 3, 1, 3), ("Z", 3, 0, 3), ("d3", 1), ("g", 2), ("b3", 1), ("b3", 0), ("ZF", 0), ("ZF", 1), ("ZF", 2),
    ("d3", 0), ("g", 3), ("ZF", 3), ("g", 4), ("H", 0), ("g", 5), ("H", 1), ("H", 2), ("AO",), ("g", 6), ("AE",),
    ("RB",), ("RD",),
)


def kernel(
    x_in, c_in, up_in, down_in, g_in,
    out_hbm, dtok_hbm, gu_hbm, gd_hbm, gg_ref,
    xo, co, ws, w_in, wz, out_ref, dtok_ref, go, xt, nc, w, relay, gr, gcol, inv_s, pre_s, dh_s, slope, hd, md_s, gs, g, xr, zs, zr,
    br, dn, b0, b1, bq0, bq1, d0, d1, dq0, dq1, stage, ga, ggp, ggr, ggx, ggy, ggz, ggc,
    send_sem, recv_sem, copy_sem,
):
    x = lax.axis_index("row")
    col = lax.axis_index("col")
    d = lax.axis_index("depth")
    y, z = lax.rem(col, NY), col // NY
    e = 1 - d

    def dev(ax=None, off=0):
        xx, yy, zz, dd = x, y, z, d
        if ax == "x":
            xx = lax.rem(x + (off + NX), NX)
        elif ax == "y":
            yy = lax.rem(y + (off + NY), NY)
        elif ax == "z":
            zz = lax.rem(z + (off + NZ), NZ)
        elif ax == "c":
            dd = e
        return (xx, zz * NY + yy, dd)

    def px(off):
        return lax.rem(x + (off + NX), NX)

    def py(off):
        return lax.rem(y + (off + NY), NY)

    def pz(off):
        return lax.rem(z + (off + NZ), NZ)

    def rows(i, size, off=0, n=None):
        return pl.ds(pl.multiple_of(i * size + off, 16), size if n is None else n)

    def lanes(i):
        return pl.ds(pl.multiple_of(i * TB, TB), TB)

    msg = Messages(send_sem, recv_sem)

    barrier = pltpu.get_barrier_semaphore()
    partners = [("x", 1), ("x", -1), ("x", 2), ("y", 1), ("y", -1), ("y", 2), ("z", 1), ("z", -1), ("c", 0)]
    for ax, off in partners:
        pl.semaphore_signal(barrier, inc=1, device_id=dev(ax, off), device_id_type=MESH)

    loads = [pltpu.make_async_copy(x_in, xo, copy_sem.at[0]), pltpu.make_async_copy(c_in, co, copy_sem.at[1])]
    for cp in loads:
        cp.start()

    @pl.when(d == 0)
    def _():
        cp = pltpu.make_async_copy(up_in, ws, copy_sem.at[2])
        cp.start()
        cp.wait()

    @pl.when(d == 1)
    def _():
        cp = pltpu.make_async_copy(down_in, ws, copy_sem.at[2])
        cp.start()
        cp.wait()

    w_in[...] = jnp.zeros_like(w_in)
    for j in range(NY):
        w_in[j, pl.ds(0, DC)] = ws[:, j * FS:j * FS + FM]
        tail = jnp.concatenate([ws[:, j * FS + FM:(j + 1) * FS].astype(F32), jnp.zeros((DC, TB - 16), F32)], axis=1)
        tail = jnp.concatenate([tail, jnp.zeros((TB - DC, TB), F32)], axis=0).T
        w_in[j, pl.ds(RP - 16, 16), pl.ds(0, 2 * TB)] = jnp.concatenate([
            jnp.concatenate([ws[RP - 16:DC, j * FS:j * FS + 2 * TB].astype(F32),
                             jnp.zeros((RP - 8 - DC, 2 * TB), F32)], axis=0),
            jnp.concatenate([tail[:8], tail[8:16]], axis=1)], axis=0).astype(BF16)
    for cp in loads:
        cp.wait()
    xt[rows(x, DX), lanes(y)] = xo[...]
    nc[1, rows(x, DX), lanes(y)] = co[...]
    gain_own = g_in[...].astype(F32).reshape(1, DX)
    gr[x] = jnp.zeros_like(gr[0])
    gr[x, :, pl.ds(0, DX)] = jnp.broadcast_to(gain_own, (8, DX))
    pl.semaphore_wait(barrier, len(partners))

    class Gather:
        def __init__(self, ref, first, second):
            self.ref, self.a, self.b = ref, first, second
            self.n1, self.n2, self.m2 = {}, {}, {}

        def at(self, a, b, half=None):
            xi, yi = (px(a), py(b)) if self.a == "x" else (px(b), py(a))
            off, n = (0, DX) if half is None else HALF[half]
            return self.ref(rows(xi, DX, off, n), lanes(yi))

        def go(self, a, b, ax, off, half=None):
            ref = self.at(a, b, half)
            return msg.start(ref, ref, dev(ax, off))

        def first(self):
            self.m1 = [self.go(0, 0, self.a, 1), self.go(0, 0, self.a, -1)]

        def second(self, a):
            self.n1[a] = [self.go(a, 0, self.b, 1), self.go(a, 0, self.b, -1)]

        def first_forward(self, s):
            self.m1[s].wait_recv()
            self.m2[s] = self.go(2 * s - 1, 0, self.a, 1 - 2 * s, s)

        def first_done(self):
            while self.m2:
                self.m2.popitem()[1].wait_recv()

        def second_step(self, a):
            if a == 2:
                self.first_done()
            self.second(a)

        def second_forward(self, a, s):
            self.n1[a][s].wait_recv()
            self.n2[a, s] = self.go(a, 2 * s - 1, self.b, 1 - 2 * s, s)

        def second_done(self):
            for a in ORDER:
                for s in (0, 1):
                    self.n2[a, s].wait_recv()

    gx = Gather(lambda r, l: xt.at[r, l], "x", "y")
    gc = Gather(lambda r, l: nc.at[1, r, l], "y", "x")

    gain_msgs = [msg.start(gr.at[x], gr.at[x], dev("x", off)) for off in (1, -1, 2)]

    def pack_parts(k, val):
        tail = jnp.concatenate([val[:, FM:], jnp.zeros((FP - DZ, FP - FM), F32)], axis=0).T[:16]
        for q in range(NY):
            g[k, q, pl.ds(0, DC)] = val[q * DC:(q + 1) * DC, :FM]
            for i in (0, 1):
                g[k, q, pl.ds(RP - 8, 8), pl.ds(i * TB, TB)] = tail[i * 8:i * 8 + 8, q * DC:q * DC + TB]

    def unpack_part(val):
        tail = jnp.concatenate([val[RP - 8:, :TB], val[RP - 8:, TB:2 * TB], jnp.zeros((TB - 16, TB), F32)], axis=0)
        return jnp.concatenate([val[:DC], tail.T[:DC]], axis=1)

    a2a, zw, wc = {}, {}, {}
    late = {0: (0, 2), 1: (1, 3)}

    def w_at(off, j):
        return wz.at[pz(off), py(ORDER[j])]

    def w_apart():
        a2a[0] = msg.start(w_in.at[py(2)], relay, dev("y", 1 - 2 * d))
        for i in (1, 2):
            a2a[i] = msg.start(w_in.at[py(ORDER[i])], wz.at[z, y], dev("y", ORDER[i]))
        wz[z, y] = w_in[y]

    def w_relay():
        a2a[0].wait_recv()
        a2a[0] = msg.start(relay, wz.at[z, py(2 * d - 1)], dev("y", 1 - 2 * d))

    def w_first(j):
        if j < 3:
            a2a[(0, 2, 1)[j]].wait_recv()
        for p in (0, 1):
            zw[0, p, j] = msg.start(w_at(0, j), w_at(0, j), dev("z", 1 - 2 * p))

    def w_forward(s, p, j):
        zw[s, p, j].wait_recv()
        ref = w_at((2 * p - 1) * (s + 1), j)
        zw[s + 1, p, j] = msg.start(ref, ref, dev("z", 1 - 2 * p))

    def w_unpack(off):
        s = abs(off) - 1
        for p in (0, 1):
            for j in range(NY):
                if (s == 3 and j in late[p]) or (s == 2 and off == (2 * p - 1) * 3 and j not in late[p]):
                    zw[s, p, j].wait_recv()
        zc = pz(off)
        r = rows(zc, DZ)
        w[d, r] = jnp.concatenate([unpack_part(wz[zc, q].astype(F32)) for q in range(NY)], axis=0).astype(BF16)
        wc[off] = msg.start(w.at[d, r], w.at[d, r], dev("c"))

    def w_done():
        for cp in wc.values():
            cp.wait_recv()

    def spread_gain(i, carry):
        column = gr[i].T[:DX, 0:1]
        gcol[i] = jnp.broadcast_to(column, (DX, TB))
        return carry

    def all_gain():
        for cp in gain_msgs:
            cp.wait_recv()
        lax.fori_loop(0, NX, spread_gain, 0)

    def normalise(off):
        yi = py(off)
        if off == 0:
            gx.first_done()
        if off == 2:
            gx.second_done()

        def square(i, acc):
            v = xt[pl.ds(pl.multiple_of(i * 160, 16), 160), lanes(yi)].astype(F32)
            return acc + jnp.sum(v * v, axis=0, keepdims=True)

        total = lax.fori_loop(0, D // 160, square, jnp.zeros((1, TB), F32))
        inv = lax.rsqrt(total / D + EPS)
        if off == 0:
            inv_s[...] = inv

        def scale(i, carry):
            xi, k = i // 5, lax.rem(i, 5)
            r = pl.ds(pl.multiple_of(i * 160, 16), 160)
            v = xt[r, lanes(yi)].astype(F32) * inv
            nc[0, r, lanes(yi)] = (v * gcol[xi, pl.ds(pl.multiple_of(k * 160, 16), 160)]).astype(BF16)
            return carry

        lax.fori_loop(0, D // 160, scale, 0)

    def pre_all():
        pre_s[...] = jnp.zeros_like(pre_s)

        def body(i, carry):
            r = rows(i, 2 * DZ)
            pre_s[...] += dot(w[0, r], nc[0, r], 0, 0)
            return carry

        lax.fori_loop(0, NZ // 2, body, 0)

    def activate():
        def body(i, carry):
            r = pl.ds(pl.multiple_of(i * 16, 16), 16)
            pre = pre_s[r]
            hd[1, r] = gelu_value(pre).astype(BF16)
            slope[r] = gelu_slope(pre)
            return carry

        lax.fori_loop(0, FS // 16, body, 0)

    def d_hidden_rows(a):
        if a == 0:
            gc.first_done()
            dh_s[...] = jnp.zeros_like(dh_s)
        if a == 2:
            gc.second_done()
        r = rows(px(a), DX)
        dh_s[...] += dot(w[1, r], nc[1, r], 0, 0)

    def d_pre():
        def body(i, acc):
            r = pl.ds(pl.multiple_of(i * 16, 16), 16)
            dpre = dh_s[r] * slope[r]
            hd[0, r] = dpre.astype(BF16)
            return acc + jnp.sum(dpre * pre_s[r], axis=0, keepdims=True)

        md_s[...] = lax.fori_loop(0, FS // 16, body, jnp.zeros((1, T), F32))

    hd[0, pl.ds(FS, FP - FS)] = jnp.zeros((FP - FS, T), BF16)
    hd[1, pl.ds(FS, FP - FS)] = jnp.zeros((FP - FS, T), BF16)
    steps = {
        "xm": gx.first, "xf": gx.first_forward, "xn": gx.second_step, "xg": gx.second_forward,
        "cm": gc.first, "cf": gc.first_forward, "cn": gc.second_step, "cg": gc.second_forward,
        "wa": w_apart, "wr": w_relay, "wz": w_first, "wf": w_forward, "wu": w_unpack, "ww": w_done,
        "gs": all_gain, "nm": normalise, "pc": pre_all, "gl": activate, "db": d_hidden_rows,
        "hp": d_pre,
    }
    for name, *where in GATHER:
        steps[name](*where)

    core = {}
    ggr[...] = jnp.zeros_like(ggr)
    g[...] = jnp.zeros_like(g)
    ones = jnp.ones((8, FP), BF16)

    def fold(k):
        core[k].wait_recv()
        total = gs[k] + xr[k].astype(F32)
        pack_parts(k, total)
        gs[k] = total

    def gain_part(k):
        zc = pz(ZORDER[k])
        v = gs[k] * w[d, rows(zc, DZ)].astype(F32)
        high = v.astype(BF16)
        low = (v - high.astype(F32)).astype(BF16)
        ggr[:, pl.ds(0, DZ)] = dot(ones, high, 1, 1) + dot(ones, low, 1, 1)
        for j in range(4):
            ggp[zc // 2, pl.ds(lax.rem(zc, 2) * 4 + j, 1), :] = ggr[0:1, j * TB:(j + 1) * TB]

    def gain_x():
        return [msg.start(ggp.at[px(off)], ggx.at[i], dev("x", off)) for i, off in enumerate((1, -1, 2))]

    def gain_y(cps):
        for cp in cps:
            cp.wait_recv()
        ggy[0] = ggp[x] + ggx[0] + ggx[1] + ggx[2]
        return [msg.start(ggy.at[0], ggy.at[1 + i], dev("y", off)) for i, off in enumerate((1, -1, 2))]

    def gain_z(cps):
        for cp in cps:
            cp.wait_recv()
        ggz[0] = ggy[0] + ggy[1] + ggy[2] + ggy[3]
        return [msg.start(ggz.at[0], ggz.at[1 + p], dev("z", 1 - 2 * p)) for p in (0, 1)]

    def gain_ring(cps, s):
        for cp in cps:
            cp.wait_recv()
        return [
            msg.start(ggz.at[2 * s - 1 + p], ggz.at[2 * s + 1 + p], dev("z", 1 - 2 * p))
            for p in ((0, 1) if s < 3 else (0,))
        ]

    def gain_c(cps):
        for cp in cps:
            cp.wait_recv()
        total = ggz[0]
        for i in range(NZ - 1):
            total = total + ggz[1 + i]
        ggc[0] = total
        return [msg.start(ggc.at[0], ggc.at[1], dev("c"))]

    def grad_chunk(k):
        r = rows(pz(ZORDER[k]), DZ)
        xt[pl.ds(k * DZ, DZ)] = dot(nc[e, r], hd[e], 1, 1).astype(BF16)
        core[k] = msg.start(xt.at[pl.ds(k * DZ, DZ)], xr.at[k], dev("c"))
        gs[k] = dot(nc[d, r], hd[d], 1, 1)

    zmsg = {}

    def z_reduce(s, p, j):
        k = 0 if s == 0 else 2 * s - 1 + p
        q = py(ORDER[j])
        val = g[k, q]
        if (s - 1, p, j) in zmsg:
            zmsg[s - 1, p, j].wait_recv()
            val = val + zr[p, s - 1, q].astype(F32)
        zs[p, s, q] = val.astype(BF16)
        zmsg[s, p, j] = msg.start(zs.at[p, s, q], zr.at[p, s, q], dev("z", 1 - 2 * p))

    back, hands = {}, {}

    def z_final(j):
        q = py(ORDER[j])
        for p in (0, 1):
            zmsg[3, p, j].wait_recv()
        val = (g[7, q] + zr[0, 3, q].astype(F32) + zr[1, 3, q].astype(F32)).astype(BF16)
        if j < 3:
            stage[j] = val
            back[j] = msg.start(stage.at[j], ga.at[d, y], dev("y", ORDER[j]))
        else:
            ga[d, y] = val
            hands[j] = msg.start(ga.at[d, y], ga.at[d, y], dev("c"))

    def hand_on(j):
        back[j].wait_recv()
        ref = ga.at[d, py(-ORDER[j])]
        hands[j] = msg.start(ref, ref, dev("c"))

    def assemble(i):
        for j in range(NY):
            go[i, :, pl.ds(j * FS, FS)] = unpack_part(ga[i, j].astype(F32))[:, :FS].astype(BF16)

    class Reduce:
        def __init__(self, ref, a, b, halves, r0, r1, q0, q1):
            self.ref, self.a, self.b, self.h = ref, a, b, halves
            self.r0, self.r1, self.q0, self.q1 = r0, r1, q0, q1
            self.p0, self.p1, self.m1 = {}, {}, {}

        def at(self, a, b):
            return (px(a), py(b)) if self.a == "x" else (px(b), py(a))

        def send0(self, b):
            i = ORDER.index(b)
            xi, yi = self.at(2, b)
            self.p0[b] = []
            for s in (0, 1):
                o, n = self.h[s]
                self.p0[b].append(msg.start(
                    self.ref.at[xi, yi, pl.ds(o, n)], self.r0.at[i, s, pl.ds(0, n)], dev(self.a, 1 - 2 * s)))

        def send1(self, b, s):
            i = ORDER.index(b)
            o, n = self.h[s]
            xi, yi = self.at(1 - 2 * s, b)
            self.p0[b][s].wait_recv()
            self.ref[xi, yi, pl.ds(o, n)] = (
                self.ref[xi, yi, pl.ds(o, n)].astype(F32) + self.r0[i, s, pl.ds(0, n)].astype(F32)
            ).astype(BF16)
            self.p1[b, s] = msg.start(self.ref.at[xi, yi], self.r1.at[i, s], dev(self.a, 1 - 2 * s))

        def sum1(self, b):
            i = ORDER.index(b)
            xi, yi = self.at(0, b)
            for s in (0, 1):
                self.p1[b, s].wait_recv()
            return self.ref[xi, yi].astype(F32) + self.r1[i, 0].astype(F32) + self.r1[i, 1].astype(F32)

        def second0(self):
            xi, yi = self.at(0, 2)
            self.ref[xi, yi] = self.sum1(2).astype(BF16)
            self.m0 = []
            for s in (0, 1):
                o, n = self.h[s]
                self.m0.append(msg.start(
                    self.ref.at[xi, yi, pl.ds(o, n)], self.q0.at[s, pl.ds(0, n)], dev(self.b, 1 - 2 * s)))

        def second1(self, s):
            b = 1 - 2 * s
            xi, yi = self.at(0, b)
            o, n = self.h[s]
            total = self.sum1(b)
            self.m0[s].wait_recv()
            self.ref[xi, yi, pl.ds(o, n)] = (
                total[o:o + n] + self.q0[s, pl.ds(0, n)].astype(F32)).astype(BF16)
            so, sn = self.h[1 - s]
            self.ref[xi, yi, pl.ds(so, sn)] = total[so:so + sn].astype(BF16)
            self.m1[s] = msg.start(self.ref.at[xi, yi], self.q1.at[s], dev(self.b, b))

        def result(self):
            total = self.sum1(0)
            for s in (0, 1):
                self.m1[s].wait_recv()
            return total + self.q1[0].astype(F32) + self.q1[1].astype(F32)

    rb = Reduce(br, "y", "x", HALF, b0, b1, bq0, bq1)
    rd = Reduce(dn, "x", "y", HALFE, d0, d1, dq0, dq1)

    def branch_block(off):
        xi = px(off)
        val = dot(w[1, rows(xi, DX)], hd[1], 1, 0).astype(BF16)
        for j in range(NY):
            br[xi, j] = val[:, j * TB:(j + 1) * TB]

    def normed_block(off):
        xi = px(off)
        val = dot(w[0, rows(xi, DX)], hd[0], 1, 0).astype(BF16)
        for j in range(NY):
            dn[xi, j, pl.ds(0, DX)] = val[:, j * TB:(j + 1) * TB]
            dn[xi, j, pl.ds(DX, EX)] = jnp.broadcast_to(
                md_s[:, j * TB:(j + 1) * TB], (EX, TB)).astype(BF16)

    def out_result():
        out_ref[...] = (xo[...].astype(F32) + rb.result()).astype(BF16)
        stores[0].start()

    def dtok_result():
        total = rd.result()
        dnorm = total[:DX]
        inv = inv_s[...]
        mean_dot = total[DX:DX + 1] / D
        unit = xo[...].astype(F32) * inv
        dtok_ref[...] = (
            co[...].astype(F32) + inv * (dnorm * gcol[x] - unit * mean_dot)
        ).astype(BF16)
        stores[1].start()

    chain = [gain_x, gain_y, gain_z, lambda m: gain_ring(m, 1), lambda m: gain_ring(m, 2),
             lambda m: gain_ring(m, 3), gain_c]
    gain = None

    def gain_step(i):
        nonlocal gain
        gain = chain[i](gain) if i else chain[0]()

    stores = [
        pltpu.make_async_copy(src, dst, copy_sem.at[i])
        for i, (src, dst) in enumerate((
            (out_ref, out_hbm), (dtok_ref, dtok_hbm), (go.at[0], gu_hbm), (go.at[1], gd_hbm)))
    ]

    def other_core():
        for j in range(NY):
            hands[j].wait_recv()
        assemble(e)

    steps = {
        "B": branch_block, "N": normed_block, "G": grad_chunk, "F": fold, "P": gain_part,
        "Z": z_reduce, "ZF": z_final, "H": hand_on, "AO": lambda: assemble(d), "AE": other_core,
        "b0": rb.send0, "b1": rb.send1, "b2": rb.second0, "b3": rb.second1, "RB": out_result,
        "d0": rd.send0, "d1": rd.send1, "d2": rd.second0, "d3": rd.second1, "RD": dtok_result,
        "g": gain_step,
    }
    for name, *where in SCHEDULE:
        steps[name](*where)

    for i in (2, 3):
        stores[i].start()
    for cp in gain:
        cp.wait_recv()
    total = jnp.where(d == 0, ggc[0], ggc[1]) * SCALE
    for i in (0, 1):
        row = jnp.concatenate([total[4 * i + j:4 * i + j + 1] for j in range(4)], axis=1)
        gg_ref[:, pl.ds(i * DZ, DZ)] = row[:, :DZ]
    gg_ref[...] = gg_ref[...] / gain_own
    assert (msg.n, msg.n_send, len(msg.pool)) == (N_MESSAGES, N_SEND, N_SEND)
    for cp in stores:
        cp.wait()


def vm(shape, dtype=BF16):
    return pltpu.VMEM(shape, dtype)


def block(x, c, up, down, g):
    spec = pl.BlockSpec(memory_space=pltpu.VMEM)
    anywhere = pl.BlockSpec(memory_space=pl.ANY)
    return pl.pallas_call(
        kernel,
        out_shape=(
            jax.ShapeDtypeStruct((DX, TB), BF16),
            jax.ShapeDtypeStruct((DX, TB), BF16),
            jax.ShapeDtypeStruct((DC, NY * FS), BF16),
            jax.ShapeDtypeStruct((DC, NY * FS), BF16),
            jax.ShapeDtypeStruct((1, DX), F32),
        ),
        in_specs=[anywhere] * 4 + [spec],
        out_specs=(anywhere,) * 4 + (spec,),
        scratch_shapes=[
            vm((DX, TB)),
            vm((DX, TB)),
            vm((DC, NY * FS)),
            vm((NY, RP, FM)),
            vm((NZ, NY, RP, FM)),
            vm((DX, TB)),
            vm((DX, TB)),
            vm((2, DC, NY * FS)),
            vm((D, T)),
            vm((2, D, T)),
            vm((2, D, FP)),
            vm((RP, FM)),
            vm((NX, 8, 896), F32),
            vm((NX, DX, TB), F32),
            vm((1, TB), F32),
            vm((FP, T), F32),
            vm((FP, T), F32),
            vm((FS, T), F32),
            vm((2, FP, T)),
            vm((1, T), F32),
            vm((NZ, DZ, FP), F32),
            vm((NZ, NY, RP, FM), F32),
            vm((NZ, DZ, FP)),
            vm((2, 4, NY, RP, FM)),
            vm((2, 4, NY, RP, FM)),
            vm((NX, NY, DX, TB)),
            vm((NX, NY, DE, TB)),
            vm((4, 2, 400, TB)),
            vm((4, 2, DX, TB)),
            vm((2, 400, TB)),
            vm((2, DX, TB)),
            vm((4, 2, 416, TB)),
            vm((4, 2, DE, TB)),
            vm((2, 416, TB)),
            vm((2, DE, TB)),
            vm((3, RP, FM)),
            vm((2, NY, RP, FM)),
            vm((NX, 8, TB), F32),
            vm((8, FP), F32),
            vm((3, 8, TB), F32),
            vm((4, 8, TB), F32),
            vm((NZ, 8, TB), F32),
            vm((2, 8, TB), F32),
            pltpu.SemaphoreType.DMA((N_SEND,)),
            pltpu.SemaphoreType.DMA((N_MESSAGES,)),
            pltpu.SemaphoreType.DMA((4,)),
        ],
        compiler_params=pltpu.CompilerParams(
            collective_id=0, has_side_effects=True, vmem_limit_bytes=60 * 2**20
        ),
    )(x, c, up, down, g)


def finish(out_in, dtok_in, gu_in, gd_in, gg_in, out_ref, dtok_ref, gu_ref, gd_ref, gg_ref):
    out_ref[...] = out_in[...]
    dtok_ref[...] = dtok_in[...]
    gu_ref[...] = gu_in[...].astype(F32) * SCALE
    gd_ref[...] = gd_in[...].astype(F32) * SCALE
    gg_ref[...] = gg_in[...].reshape(DX)


def on_device(tokens, gain, w_up, w_down, cotangent):
    parts = block(tokens.T, cotangent.T, w_up, w_down.T, gain)
    spec = pl.BlockSpec(memory_space=pltpu.VMEM)
    out, d_tokens, grad_up, grad_down, grad_gain = pl.pallas_call(
        finish,
        out_shape=(
            jax.ShapeDtypeStruct((DX, TB), BF16),
            jax.ShapeDtypeStruct((DX, TB), BF16),
            jax.ShapeDtypeStruct((DC, NY * FS), F32),
            jax.ShapeDtypeStruct((DC, NY * FS), F32),
            jax.ShapeDtypeStruct((DX,), F32),
        ),
        in_specs=[spec] * 5,
        out_specs=(spec,) * 5,
    )(*parts)
    return out.T, d_tokens.T, grad_up, grad_down.T, grad_gain


def solution(mesh):
    in_specs = (
        P(("depth", "col"), "row"),
        P("row"),
        P("col", "row"),
        P("row", "col"),
        P(("depth", "col"), "row"),
    )
    out_specs = (
        P(("depth", "col"), "row"),
        P(("depth", "col"), "row"),
        P("col", "row"),
        P("row", "col"),
        P("row"),
    )
    return jax.shard_map(
        on_device, mesh=mesh, in_specs=in_specs, out_specs=out_specs, check_vma=False
    )
```

```python
import math

import jax
import jax.numpy as jnp
from jax import lax
from jax.experimental import pallas as pl
from jax.experimental.pallas import tpu as pltpu
from jax.sharding import PartitionSpec as P

EPS = 1e-06
MESH = pl.DeviceIdType.MESH
F32, BF16 = jnp.float32, jnp.bfloat16

NX, NY, NZ = 4, 4, 8
D, FF, TOK = 3200, 6400, 8192
DX = D // NX
TB = 128
T = NY * TB
DZ = D // NZ
DC = D // (NY * NZ)
FS = FF // (NX * NY)
FP = 512
RP = 112
EX = 16
DE = DX + EX
FM = 384
HALF = ((0, 400), (400, 400))
HALFE = ((0, 400), (400, 416))
ORDER = (2, 1, -1, 0)
ZORDER = (4, 3, -3, 2, -2, 1, -1, 0)
SCALE = TOK ** (-0.5)


def gelu_value(pre):
    return 0.5 * pre * (1.0 + lax.erf(pre / math.sqrt(2.0)))


def gelu_slope(pre):
    return 0.5 * (1.0 + lax.erf(pre / math.sqrt(2.0))) + pre * jnp.exp(
        -0.5 * pre * pre
    ) / math.sqrt(2.0 * math.pi)


def dot(left, right, left_dim, right_dim):
    return lax.dot_general(
        left, right, (((left_dim,), (right_dim,)), ((), ())), preferred_element_type=F32
    )


class Message:
    def __init__(self, copy, pool, i):
        self.copy, self.pool, self.i = copy, pool, i

    def wait_recv(self):
        self.copy.wait_recv()
        self.copy.wait_send()
        self.pool.append(self.i)


class Messages:
    def __init__(self, send, recv):
        self.send, self.recv, self.n, self.n_send, self.pool = send, recv, 0, 0, []

    def start(self, src, dst, device):
        if self.pool:
            i = self.pool.pop(0)
        else:
            i = self.n_send
            self.n_send += 1
        cp = pltpu.make_async_remote_copy(
            src_ref=src, dst_ref=dst, send_sem=self.send.at[i], recv_sem=self.recv.at[self.n],
            device_id=device, device_id_type=MESH,
        )
        self.n += 1
        cp.start()
        return Message(cp, self.pool, i)


N_MESSAGES, N_SEND = 180, 29

GATHER = (
    ("wa",), ("xm",), ("cm",), ("wz", 3), ("xn", 0), ("cn", 0), ("gs",), ("wr",), ("wz", 1), ("wf", 0, 0, 3),
    ("wf", 0, 1, 3), ("wz", 2), ("xf", 0), ("xf", 1), ("xn", 1), ("xn", -1), ("wf", 0, 0, 1), ("wf", 0, 1, 1),
    ("cf", 0), ("cf", 1), ("cn", 1), ("wf", 1, 1, 3), ("cn", -1), ("wf", 1, 0, 3), ("cg", 0, 0), ("cg", 0, 1),
    ("wf", 0, 0, 2), ("wf", 0, 1, 2), ("wf", 1, 0, 1), ("wf", 1, 1, 1), ("xn", 2), ("nm", 0), ("xg", 0, 0),
    ("xg", 0, 1), ("wz", 0), ("wu", 0), ("wf", 2, 1, 3), ("wf", 1, 0, 2), ("wf", 1, 1, 2), ("cg", 1, 0), ("cg", 1, 1),
    ("wf", 2, 1, 1), ("xg", 1, 0), ("xg", 1, 1), ("wf", 0, 0, 0), ("wf", 0, 1, 0), ("wu", -1), ("wu", 1),
    ("cg", -1, 0), ("cg", -1, 1), ("wf", 2, 0, 2), ("xg", -1, 0), ("xg", -1, 1), ("wf", 1, 0, 0), ("wu", -2),
    ("cn", 2), ("wf", 1, 1, 0), ("wf", 2, 0, 0), ("wu", 2), ("wu", -3), ("xg", 2, 0), ("xg", 2, 1), ("nm", -1),
    ("nm", 1), ("wu", 3), ("wu", 4), ("cg", 2, 0), ("cg", 2, 1), ("ww",), ("db", 0), ("db", -1), ("db", 1), ("db", 2),
    ("nm", 2), ("pc",), ("gl",), ("hp",),
)

SCHEDULE = (
    ("G", 0), ("B", 2), ("b0", 2), ("N", 2), ("d0", 2), ("G", 1), ("B", 1), ("B", -1), ("G", 2), ("b0", -1), ("G", 7),
    ("F", 0), ("Z", 0, 0, 0), ("Z", 0, 1, 1), ("Z", 0, 0, 2), ("G", 5), ("G", 6), ("b1", 2, 1), ("b1", 2, 0),
    ("F", 1), ("Z", 1, 0, 1), ("b0", 1), ("d0", -1), ("G", 4), ("N", 1), ("F", 2), ("Z", 1, 1, 0), ("Z", 1, 1, 2),
    ("G", 3), ("b1", -1, 1), ("F", 7), ("Z", 1, 0, 0), ("Z", 1, 1, 1), ("d0", 1), ("b1", -1, 0), ("N", -1), ("F", 5),
    ("Z", 0, 1, 3), ("B", 0), ("Z", 1, 0, 2), ("F", 6), ("P", 6), ("d1", 2, 0), ("P", 2), ("P", 0), ("F", 4),
    ("Z", 2, 1, 0), ("P", 4), ("P", 5), ("P", 1), ("b2",), ("F", 3), ("P", 3), ("Z", 2, 0, 1), ("P", 7), ("g", 0),
    ("Z", 2, 1, 2), ("Z", 1, 0, 3), ("Z", 2, 0, 0), ("d1", 2, 1), ("d0", 0), ("N", 0), ("b1", 1, 0), ("b1", 1, 1),
    ("b0", 0), ("d1", -1, 1), ("d1", 1, 1), ("Z", 2, 1, 1), ("d1", 1, 0), ("d1", -1, 0), ("Z", 2, 0, 2),
    ("Z", 1, 1, 3), ("Z", 3, 0, 1), ("b3", 1), ("Z", 3, 1, 0), ("Z", 2, 0, 3), ("g", 1), ("Z", 3, 1, 2),
    ("Z", 3, 0, 0), ("d2",), ("d1", 0, 0), ("Z", 3, 1, 1), ("Z", 3, 0, 2), ("b3", 0), ("d1", 0, 1), ("Z", 2, 1, 3),
    ("b1", 0, 1), ("b1", 0, 0), ("g", 2), ("Z", 3, 0, 3), ("ZF", 0), ("ZF", 1), ("ZF", 2), ("g", 3), ("d3", 1),
    ("Z", 3, 1, 3), ("d3", 0), ("g", 4), ("H", 2), ("H", 0), ("g", 5), ("ZF", 3), ("H", 1), ("AO",), ("g", 6),
    ("RB",), ("AE",), ("RD",),
)


def kernel(
    x_in, c_in, up_in, down_in, g_in,
    out_hbm, dtok_hbm, gu_hbm, gd_hbm, gg_ref,
    xo, co, ws, w_in, wz, out_ref, dtok_ref, go, xt, nc, w, relay, gr, gcol, inv_s, pre_s, dh_s, slope, hd, md_s, gs, g, xr, zr,
    br, dn, b0, b1, bq0, bq1, d0, d1, dq0, dq1, stage, ga, ggp, ggr, ggx, ggy, ggz, ggc,
    send_sem, recv_sem, copy_sem,
):
    x = lax.axis_index("row")
    col = lax.axis_index("col")
    d = lax.axis_index("depth")
    y, z = lax.rem(col, NY), col // NY
    e = 1 - d

    def dev(ax=None, off=0):
        xx, yy, zz, dd = x, y, z, d
        if ax == "x":
            xx = lax.rem(x + (off + NX), NX)
        elif ax == "y":
            yy = lax.rem(y + (off + NY), NY)
        elif ax == "z":
            zz = lax.rem(z + (off + NZ), NZ)
        elif ax == "c":
            dd = e
        return (xx, zz * NY + yy, dd)

    def px(off):
        return lax.rem(x + (off + NX), NX)

    def py(off):
        return lax.rem(y + (off + NY), NY)

    def pz(off):
        return lax.rem(z + (off + NZ), NZ)

    def rows(i, size, off=0, n=None):
        return pl.ds(pl.multiple_of(i * size + off, 16), size if n is None else n)

    def lanes(i):
        return pl.ds(pl.multiple_of(i * TB, TB), TB)

    msg = Messages(send_sem, recv_sem)

    barrier = pltpu.get_barrier_semaphore()
    partners = [("x", 1), ("x", -1), ("x", 2), ("y", 1), ("y", -1), ("y", 2), ("z", 1), ("z", -1), ("c", 0)]
    for ax, off in partners:
        pl.semaphore_signal(barrier, inc=1, device_id=dev(ax, off), device_id_type=MESH)

    loads = [pltpu.make_async_copy(x_in, xo, copy_sem.at[0]), pltpu.make_async_copy(c_in, co, copy_sem.at[1])]
    for cp in loads:
        cp.start()

    @pl.when(d == 0)
    def _():
        cp = pltpu.make_async_copy(up_in, ws, copy_sem.at[2])
        cp.start()
        cp.wait()

    @pl.when(d == 1)
    def _():
        cp = pltpu.make_async_copy(down_in, ws, copy_sem.at[2])
        cp.start()
        cp.wait()

    w_in[...] = jnp.zeros_like(w_in)
    for j in range(NY):
        w_in[j, pl.ds(0, DC)] = ws[:, j * FS:j * FS + FM]
        tail = jnp.concatenate([ws[:, j * FS + FM:(j + 1) * FS].astype(F32), jnp.zeros((DC, TB - 16), F32)], axis=1)
        tail = jnp.concatenate([tail, jnp.zeros((TB - DC, TB), F32)], axis=0).T
        w_in[j, pl.ds(RP - 16, 16), pl.ds(0, 2 * TB)] = jnp.concatenate([
            jnp.concatenate([ws[RP - 16:DC, j * FS:j * FS + 2 * TB].astype(F32),
                             jnp.zeros((RP - 8 - DC, 2 * TB), F32)], axis=0),
            jnp.concatenate([tail[:8], tail[8:16]], axis=1)], axis=0).astype(BF16)
    for cp in loads:
        cp.wait()
    xt[rows(x, DX), lanes(y)] = xo[...]
    nc[1, rows(x, DX), lanes(y)] = co[...]
    gain_own = g_in[...].astype(F32).reshape(1, DX)
    gr[x] = jnp.zeros_like(gr[0])
    gr[x, :, pl.ds(0, DX)] = jnp.broadcast_to(gain_own, (8, DX))
    pl.semaphore_wait(barrier, len(partners))

    class Gather:
        def __init__(self, ref, first, second):
            self.ref, self.a, self.b = ref, first, second
            self.n1, self.n2, self.m2 = {}, {}, {}

        def at(self, a, b, half=None):
            xi, yi = (px(a), py(b)) if self.a == "x" else (px(b), py(a))
            off, n = (0, DX) if half is None else HALF[half]
            return self.ref(rows(xi, DX, off, n), lanes(yi))

        def go(self, a, b, ax, off, half=None):
            ref = self.at(a, b, half)
            return msg.start(ref, ref, dev(ax, off))

        def first(self):
            self.m1 = [self.go(0, 0, self.a, 1), self.go(0, 0, self.a, -1)]

        def second(self, a):
            self.n1[a] = [self.go(a, 0, self.b, 1), self.go(a, 0, self.b, -1)]

        def first_forward(self, s):
            self.m1[s].wait_recv()
            self.m2[s] = self.go(2 * s - 1, 0, self.a, 1 - 2 * s, s)

        def first_done(self):
            while self.m2:
                self.m2.popitem()[1].wait_recv()

        def second_step(self, a):
            if a == 2:
                self.first_done()
            self.second(a)

        def second_forward(self, a, s):
            self.n1[a][s].wait_recv()
            self.n2[a, s] = self.go(a, 2 * s - 1, self.b, 1 - 2 * s, s)

        def second_done(self):
            for a in ORDER:
                for s in (0, 1):
                    self.n2[a, s].wait_recv()

    gx = Gather(lambda r, l: xt.at[r, l], "x", "y")
    gc = Gather(lambda r, l: nc.at[1, r, l], "y", "x")

    gain_msgs = [msg.start(gr.at[x], gr.at[x], dev("x", off)) for off in (1, -1, 2)]

    def pack_parts(k, val):
        tail = jnp.concatenate([val[:, FM:], jnp.zeros((FP - DZ, FP - FM), F32)], axis=0).T[:16]
        for q in range(NY):
            g[k, q, pl.ds(0, DC)] = val[q * DC:(q + 1) * DC, :FM]
            for i in (0, 1):
                g[k, q, pl.ds(RP - 8, 8), pl.ds(i * TB, TB)] = tail[i * 8:i * 8 + 8, q * DC:q * DC + TB]

    def unpack_part(val):
        tail = jnp.concatenate([val[RP - 8:, :TB], val[RP - 8:, TB:2 * TB], jnp.zeros((TB - 16, TB), F32)], axis=0)
        return jnp.concatenate([val[:DC], tail.T[:DC]], axis=1)

    a2a, zw, wc = {}, {}, {}
    late = {0: (0, 2), 1: (1, 3)}

    def w_at(off, j):
        return wz.at[pz(off), py(ORDER[j])]

    def w_apart():
        a2a[0] = msg.start(w_in.at[py(2)], relay, dev("y", 1 - 2 * d))
        for i in (1, 2):
            a2a[i] = msg.start(w_in.at[py(ORDER[i])], wz.at[z, y], dev("y", ORDER[i]))
        wz[z, y] = w_in[y]

    def w_relay():
        a2a[0].wait_recv()
        a2a[0] = msg.start(relay, wz.at[z, py(2 * d - 1)], dev("y", 1 - 2 * d))

    def w_first(j):
        if j < 3:
            a2a[(0, 2, 1)[j]].wait_recv()
        for p in (0, 1):
            zw[0, p, j] = msg.start(w_at(0, j), w_at(0, j), dev("z", 1 - 2 * p))

    def w_forward(s, p, j):
        zw[s, p, j].wait_recv()
        ref = w_at((2 * p - 1) * (s + 1), j)
        zw[s + 1, p, j] = msg.start(ref, ref, dev("z", 1 - 2 * p))

    def w_unpack(off):
        s = abs(off) - 1
        for p in (0, 1):
            for j in range(NY):
                if (s == 3 and j in late[p]) or (s == 2 and off == (2 * p - 1) * 3 and j not in late[p]):
                    zw[s, p, j].wait_recv()
        zc = pz(off)
        r = rows(zc, DZ)
        w[d, r] = jnp.concatenate([unpack_part(wz[zc, q].astype(F32)) for q in range(NY)], axis=0).astype(BF16)
        wc[off] = msg.start(w.at[d, r], w.at[d, r], dev("c"))

    def w_done():
        for cp in wc.values():
            cp.wait_recv()

    def spread_gain(i, carry):
        column = gr[i].T[:DX, 0:1]
        gcol[i] = jnp.broadcast_to(column, (DX, TB))
        return carry

    def all_gain():
        for cp in gain_msgs:
            cp.wait_recv()
        lax.fori_loop(0, NX, spread_gain, 0)

    def normalise(off):
        yi = py(off)
        if off == 0:
            gx.first_done()
        if off == 2:
            gx.second_done()

        def square(i, acc):
            v = xt[pl.ds(pl.multiple_of(i * 160, 16), 160), lanes(yi)].astype(F32)
            return acc + jnp.sum(v * v, axis=0, keepdims=True)

        total = lax.fori_loop(0, D // 160, square, jnp.zeros((1, TB), F32))
        inv = lax.rsqrt(total / D + EPS)
        if off == 0:
            inv_s[...] = inv

        def scale(i, carry):
            xi, k = i // 5, lax.rem(i, 5)
            r = pl.ds(pl.multiple_of(i * 160, 16), 160)
            v = xt[r, lanes(yi)].astype(F32) * inv
            nc[0, r, lanes(yi)] = (v * gcol[xi, pl.ds(pl.multiple_of(k * 160, 16), 160)]).astype(BF16)
            return carry

        lax.fori_loop(0, D // 160, scale, 0)

    def pre_all():
        pre_s[...] = jnp.zeros_like(pre_s)

        def body(i, carry):
            r = rows(i, 2 * DZ)
            pre_s[...] += dot(w[0, r], nc[0, r], 0, 0)
            return carry

        lax.fori_loop(0, NZ // 2, body, 0)

    def activate():
        def body(i, carry):
            r = pl.ds(pl.multiple_of(i * 16, 16), 16)
            pre = pre_s[r]
            hd[1, r] = gelu_value(pre).astype(BF16)
            slope[r] = gelu_slope(pre)
            return carry

        lax.fori_loop(0, FS // 16, body, 0)

    def d_hidden_rows(a):
        if a == 0:
            gc.first_done()
            dh_s[...] = jnp.zeros_like(dh_s)
        if a == 2:
            gc.second_done()
        r = rows(px(a), DX)
        dh_s[...] += dot(w[1, r], nc[1, r], 0, 0)

    def d_pre():
        def body(i, acc):
            r = pl.ds(pl.multiple_of(i * 16, 16), 16)
            dpre = dh_s[r] * slope[r]
            hd[0, r] = dpre.astype(BF16)
            return acc + jnp.sum(dpre * pre_s[r], axis=0, keepdims=True)

        md_s[...] = lax.fori_loop(0, FS // 16, body, jnp.zeros((1, T), F32))

    hd[0, pl.ds(FS, FP - FS)] = jnp.zeros((FP - FS, T), BF16)
    hd[1, pl.ds(FS, FP - FS)] = jnp.zeros((FP - FS, T), BF16)
    steps = {
        "xm": gx.first, "xf": gx.first_forward, "xn": gx.second_step, "xg": gx.second_forward,
        "cm": gc.first, "cf": gc.first_forward, "cn": gc.second_step, "cg": gc.second_forward,
        "wa": w_apart, "wr": w_relay, "wz": w_first, "wf": w_forward, "wu": w_unpack, "ww": w_done,
        "gs": all_gain, "nm": normalise, "pc": pre_all, "gl": activate, "db": d_hidden_rows,
        "hp": d_pre,
    }
    for name, *where in GATHER:
        steps[name](*where)

    core = {}
    ggr[...] = jnp.zeros_like(ggr)
    g[...] = jnp.zeros_like(g)
    ones = jnp.ones((8, FP), BF16)

    def fold(k):
        core[k].wait_recv()
        total = gs[k] + xr[k].astype(F32)
        pack_parts(k, total)
        gs[k] = total

    def gain_part(k):
        zc = pz(ZORDER[k])
        v = gs[k] * w[d, rows(zc, DZ)].astype(F32)
        high = v.astype(BF16)
        low = (v - high.astype(F32)).astype(BF16)
        ggr[:, pl.ds(0, DZ)] = dot(ones, high, 1, 1) + dot(ones, low, 1, 1)
        for j in range(4):
            ggp[zc // 2, pl.ds(lax.rem(zc, 2) * 4 + j, 1), :] = ggr[0:1, j * TB:(j + 1) * TB]

    def gain_x():
        return [msg.start(ggp.at[px(off)], ggx.at[i], dev("x", off)) for i, off in enumerate((1, -1, 2))]

    def gain_y(cps):
        for cp in cps:
            cp.wait_recv()
        ggy[0] = ggp[x] + ggx[0] + ggx[1] + ggx[2]
        return [msg.start(ggy.at[0], ggy.at[1 + i], dev("y", off)) for i, off in enumerate((1, -1, 2))]

    def gain_z(cps):
        for cp in cps:
            cp.wait_recv()
        ggz[0] = ggy[0] + ggy[1] + ggy[2] + ggy[3]
        return [msg.start(ggz.at[0], ggz.at[1 + p], dev("z", 1 - 2 * p)) for p in (0, 1)]

    def gain_ring(cps, s):
        for cp in cps:
            cp.wait_recv()
        return [
            msg.start(ggz.at[2 * s - 1 + p], ggz.at[2 * s + 1 + p], dev("z", 1 - 2 * p))
            for p in ((0, 1) if s < 3 else (0,))
        ]

    def gain_c(cps):
        for cp in cps:
            cp.wait_recv()
        total = ggz[0]
        for i in range(NZ - 1):
            total = total + ggz[1 + i]
        ggc[0] = total
        return [msg.start(ggc.at[0], ggc.at[1], dev("c"))]

    def grad_chunk(k):
        r = rows(pz(ZORDER[k]), DZ)
        xt[pl.ds(k * DZ, DZ)] = dot(nc[e, r], hd[e], 1, 1).astype(BF16)
        core[k] = msg.start(xt.at[pl.ds(k * DZ, DZ)], xr.at[k], dev("c"))
        gs[k] = dot(nc[d, r], hd[d], 1, 1)

    zmsg = {}

    def z_reduce(s, p, j):
        k = 0 if s == 0 else 2 * s - 1 + p
        q = py(ORDER[j])
        val = g[k, q]
        if (s - 1, p, j) in zmsg:
            zmsg[s - 1, p, j].wait_recv()
            val = val + zr[p, s - 1, q].astype(F32)
        wz[4 * p + s, q] = val.astype(BF16)
        zmsg[s, p, j] = msg.start(wz.at[4 * p + s, q], zr.at[p, s, q], dev("z", 1 - 2 * p))

    back, hands = {}, {}

    def z_final(j):
        q = py(ORDER[j])
        for p in (0, 1):
            zmsg[3, p, j].wait_recv()
        val = (g[7, q] + zr[0, 3, q].astype(F32) + zr[1, 3, q].astype(F32)).astype(BF16)
        if j < 3:
            stage[j] = val
            back[j] = msg.start(stage.at[j], ga.at[d, y], dev("y", ORDER[j]))
        else:
            ga[d, y] = val
            hands[j] = msg.start(ga.at[d, y], ga.at[d, y], dev("c"))

    def hand_on(j):
        back[j].wait_recv()
        ref = ga.at[d, py(-ORDER[j])]
        hands[j] = msg.start(ref, ref, dev("c"))

    def assemble(i):
        for j in range(NY):
            go[i, :, pl.ds(j * FS, FS)] = unpack_part(ga[i, j].astype(F32))[:, :FS].astype(BF16)

    class Reduce:
        def __init__(self, ref, a, b, halves, r0, r1, q0, q1):
            self.ref, self.a, self.b, self.h = ref, a, b, halves
            self.r0, self.r1, self.q0, self.q1 = r0, r1, q0, q1
            self.p0, self.p1, self.m1 = {}, {}, {}

        def at(self, a, b):
            return (px(a), py(b)) if self.a == "x" else (px(b), py(a))

        def send0(self, b):
            i = ORDER.index(b)
            xi, yi = self.at(2, b)
            self.p0[b] = []
            for s in (0, 1):
                o, n = self.h[s]
                self.p0[b].append(msg.start(
                    self.ref.at[xi, yi, pl.ds(o, n)], self.r0.at[i, s, pl.ds(0, n)], dev(self.a, 1 - 2 * s)))

        def send1(self, b, s):
            i = ORDER.index(b)
            o, n = self.h[s]
            xi, yi = self.at(1 - 2 * s, b)
            self.p0[b][s].wait_recv()
            self.ref[xi, yi, pl.ds(o, n)] = (
                self.ref[xi, yi, pl.ds(o, n)].astype(F32) + self.r0[i, s, pl.ds(0, n)].astype(F32)
            ).astype(BF16)
            self.p1[b, s] = msg.start(self.ref.at[xi, yi], self.r1.at[i, s], dev(self.a, 1 - 2 * s))

        def sum1(self, b):
            i = ORDER.index(b)
            xi, yi = self.at(0, b)
            for s in (0, 1):
                self.p1[b, s].wait_recv()
            return self.ref[xi, yi].astype(F32) + self.r1[i, 0].astype(F32) + self.r1[i, 1].astype(F32)

        def second0(self):
            xi, yi = self.at(0, 2)
            self.ref[xi, yi] = self.sum1(2).astype(BF16)
            self.m0 = []
            for s in (0, 1):
                o, n = self.h[s]
                self.m0.append(msg.start(
                    self.ref.at[xi, yi, pl.ds(o, n)], self.q0.at[s, pl.ds(0, n)], dev(self.b, 1 - 2 * s)))

        def second1(self, s):
            b = 1 - 2 * s
            xi, yi = self.at(0, b)
            o, n = self.h[s]
            total = self.sum1(b)
            self.m0[s].wait_recv()
            self.ref[xi, yi, pl.ds(o, n)] = (
                total[o:o + n] + self.q0[s, pl.ds(0, n)].astype(F32)).astype(BF16)
            so, sn = self.h[1 - s]
            self.ref[xi, yi, pl.ds(so, sn)] = total[so:so + sn].astype(BF16)
            self.m1[s] = msg.start(self.ref.at[xi, yi], self.q1.at[s], dev(self.b, b))

        def result(self):
            total = self.sum1(0)
            for s in (0, 1):
                self.m1[s].wait_recv()
            return total + self.q1[0].astype(F32) + self.q1[1].astype(F32)

    rb = Reduce(br, "y", "x", HALF, b0, b1, bq0, bq1)
    rd = Reduce(dn, "x", "y", HALFE, d0, d1, dq0, dq1)

    def branch_block(off):
        xi = px(off)
        val = dot(w[1, rows(xi, DX)], hd[1], 1, 0).astype(BF16)
        for j in range(NY):
            br[xi, j] = val[:, j * TB:(j + 1) * TB]

    def normed_block(off):
        xi = px(off)
        val = dot(w[0, rows(xi, DX)], hd[0], 1, 0).astype(BF16)
        for j in range(NY):
            dn[xi, j, pl.ds(0, DX)] = val[:, j * TB:(j + 1) * TB]
            dn[xi, j, pl.ds(DX, EX)] = jnp.broadcast_to(
                md_s[:, j * TB:(j + 1) * TB], (EX, TB)).astype(BF16)

    def out_result():
        out_ref[...] = (xo[...].astype(F32) + rb.result()).astype(BF16)
        stores[0].start()

    def dtok_result():
        total = rd.result()
        dnorm = total[:DX]
        inv = inv_s[...]
        mean_dot = total[DX:DX + 1] / D
        unit = xo[...].astype(F32) * inv
        dtok_ref[...] = (
            co[...].astype(F32) + inv * (dnorm * gcol[x] - unit * mean_dot)
        ).astype(BF16)
        stores[1].start()

    chain = [gain_x, gain_y, gain_z, lambda m: gain_ring(m, 1), lambda m: gain_ring(m, 2),
             lambda m: gain_ring(m, 3), gain_c]
    gain = None

    def gain_step(i):
        nonlocal gain
        gain = chain[i](gain) if i else chain[0]()

    stores = [
        pltpu.make_async_copy(src, dst, copy_sem.at[i])
        for i, (src, dst) in enumerate((
            (out_ref, out_hbm), (dtok_ref, dtok_hbm), (go.at[0], gu_hbm), (go.at[1], gd_hbm)))
    ]

    def other_core():
        for j in range(NY):
            hands[j].wait_recv()
        assemble(e)

    steps = {
        "B": branch_block, "N": normed_block, "G": grad_chunk, "F": fold, "P": gain_part,
        "Z": z_reduce, "ZF": z_final, "H": hand_on, "AO": lambda: assemble(d), "AE": other_core,
        "b0": rb.send0, "b1": rb.send1, "b2": rb.second0, "b3": rb.second1, "RB": out_result,
        "d0": rd.send0, "d1": rd.send1, "d2": rd.second0, "d3": rd.second1, "RD": dtok_result,
        "g": gain_step,
    }
    for name, *where in SCHEDULE:
        steps[name](*where)

    for i in (2, 3):
        stores[i].start()
    for cp in gain:
        cp.wait_recv()
    total = jnp.where(d == 0, ggc[0], ggc[1]) * SCALE
    for i in (0, 1):
        row = jnp.concatenate([total[4 * i + j:4 * i + j + 1] for j in range(4)], axis=1)
        gg_ref[:, pl.ds(i * DZ, DZ)] = row[:, :DZ]
    gg_ref[...] = gg_ref[...] / gain_own
    assert (msg.n, msg.n_send, len(msg.pool)) == (N_MESSAGES, N_SEND, N_SEND)
    for cp in stores:
        cp.wait()


def vm(shape, dtype=BF16):
    return pltpu.VMEM(shape, dtype)


def block(x, c, up, down, g):
    spec = pl.BlockSpec(memory_space=pltpu.VMEM)
    anywhere = pl.BlockSpec(memory_space=pl.ANY)
    return pl.pallas_call(
        kernel,
        out_shape=(
            jax.ShapeDtypeStruct((DX, TB), BF16),
            jax.ShapeDtypeStruct((DX, TB), BF16),
            jax.ShapeDtypeStruct((DC, NY * FS), BF16),
            jax.ShapeDtypeStruct((DC, NY * FS), BF16),
            jax.ShapeDtypeStruct((1, DX), F32),
        ),
        in_specs=[anywhere] * 4 + [spec],
        out_specs=(anywhere,) * 4 + (spec,),
        scratch_shapes=[
            vm((DX, TB)),
            vm((DX, TB)),
            vm((DC, NY * FS)),
            vm((NY, RP, FM)),
            vm((NZ, NY, RP, FM)),
            vm((DX, TB)),
            vm((DX, TB)),
            vm((2, DC, NY * FS)),
            vm((D, T)),
            vm((2, D, T)),
            vm((2, D, FP)),
            vm((RP, FM)),
            vm((NX, 8, 896), F32),
            vm((NX, DX, TB), F32),
            vm((1, TB), F32),
            vm((FP, T), F32),
            vm((FP, T), F32),
            vm((FS, T), F32),
            vm((2, FP, T)),
            vm((1, T), F32),
            vm((NZ, DZ, FP), F32),
            vm((NZ, NY, RP, FM), F32),
            vm((NZ, DZ, FP)),
            vm((2, 4, NY, RP, FM)),
            vm((NX, NY, DX, TB)),
            vm((NX, NY, DE, TB)),
            vm((4, 2, 400, TB)),
            vm((4, 2, DX, TB)),
            vm((2, 400, TB)),
            vm((2, DX, TB)),
            vm((4, 2, 416, TB)),
            vm((4, 2, DE, TB)),
            vm((2, 416, TB)),
            vm((2, DE, TB)),
            vm((3, RP, FM)),
            vm((2, NY, RP, FM)),
            vm((NX, 8, TB), F32),
            vm((8, FP), F32),
            vm((3, 8, TB), F32),
            vm((4, 8, TB), F32),
            vm((NZ, 8, TB), F32),
            vm((2, 8, TB), F32),
            pltpu.SemaphoreType.DMA((N_SEND,)),
            pltpu.SemaphoreType.DMA((N_MESSAGES,)),
            pltpu.SemaphoreType.DMA((4,)),
        ],
        compiler_params=pltpu.CompilerParams(
            collective_id=0, has_side_effects=True, vmem_limit_bytes=60 * 2**20
        ),
    )(x, c, up, down, g)


def finish(out_in, dtok_in, gu_in, gd_in, gg_in, out_ref, dtok_ref, gu_ref, gd_ref, gg_ref):
    out_ref[...] = out_in[...]
    dtok_ref[...] = dtok_in[...]
    gu_ref[...] = gu_in[...].astype(F32) * SCALE
    gd_ref[...] = gd_in[...].astype(F32) * SCALE
    gg_ref[...] = gg_in[...].reshape(DX)


def on_device(tokens, gain, w_up, w_down, cotangent):
    parts = block(tokens.T, cotangent.T, w_up, w_down.T, gain)
    spec = pl.BlockSpec(memory_space=pltpu.VMEM)
    out, d_tokens, grad_up, grad_down, grad_gain = pl.pallas_call(
        finish,
        out_shape=(
            jax.ShapeDtypeStruct((DX, TB), BF16),
            jax.ShapeDtypeStruct((DX, TB), BF16),
            jax.ShapeDtypeStruct((DC, NY * FS), F32),
            jax.ShapeDtypeStruct((DC, NY * FS), F32),
            jax.ShapeDtypeStruct((DX,), F32),
        ),
        in_specs=[spec] * 5,
        out_specs=(spec,) * 5,
    )(*parts)
    return out.T, d_tokens.T, grad_up, grad_down.T, grad_gain


def solution(mesh):
    in_specs = (
        P(("depth", "col"), "row"),
        P("row"),
        P("col", "row"),
        P("row", "col"),
        P(("depth", "col"), "row"),
    )
    out_specs = (
        P(("depth", "col"), "row"),
        P(("depth", "col"), "row"),
        P("col", "row"),
        P("row", "col"),
        P("row"),
    )
    return jax.shard_map(
        on_device, mesh=mesh, in_specs=in_specs, out_specs=out_specs, check_vma=False
    )
```
